32 devices in a mesh: dp: 16 (over z, y, core), fsdp: 2 (over x).
Axes of the slice: x: 2, y: 2, z: 4, core: 2. Of those that a mesh axis runs over, the one named last changes fastest.
Arguments:
- tokens: float32 [64, 1088, 1024], P(('dp', 'fsdp')), may hold values from -6 to 6
- cotangent: float32 [64, 1088, 1024], P(('dp', 'fsdp')), may hold values from -6 to 6
- group_ids: int32 [64], P(('dp', 'fsdp')), may hold values from 0 to 7
- counts: int32 [32], P(('dp', 'fsdp')), may hold values from 1 to 2, as said below
- w_qkv: float32 [1024, 3072], P('fsdp'), may hold values from -0.1875 to 0.1875
- w_proj: float32 [1024, 1024], P('fsdp'), may hold values from -0.75 to 0.75
- w_up: float32 [1024, 4096], P('fsdp'), may hold values from -0.1875 to 0.1875
- w_down: float32 [4096, 1024], P('fsdp'), may hold values from -0.09375 to 0.09375
- gains: float32 [4, 1024], P(None, 'fsdp'), may hold values from 0.25 to 1.75
- table: float32 [8, 1024], P(None, 'fsdp'), may hold values from -3 to 3
Outputs:
- output: float32 [64, 1088, 1024], P(('dp', 'fsdp'))
- grad_tokens: float32 [64, 1088, 1024], P(('dp', 'fsdp'))
- grad_qkv: float32 [1024, 3072], P('fsdp')
- grad_proj: float32 [1024, 1024], P('fsdp')
- grad_up: float32 [1024, 4096], P('fsdp')
- grad_down: float32 [4096, 1024], P('fsdp')
- grad_gains: float32 [4, 1024], P(None, 'fsdp')
- grad_table: float32 [8, 1024], P(None, 'fsdp')
The draws below stay inside these ranges and needn't reach their ends.
Inputs may be any that keep to these rules, and one draw needn't show every extreme that they name: `counts`: the number of live slots of each device, which are its first ones; some device holds 2 and some holds 1.
All inputs are finite; a program needn't handle non-finite values.
Results may differ from the reference program's by a relative error of at most 0.012.
Values may be sent and summed in bfloat16 or wider, within the bound.
No kernel may reach another device: no remote copies, remote signals or barrier semaphores. Data moves between devices by JAX's collectives and lax.ppermute only.
A program may use at most 704 MiB of HBM per device.

```python
import math
import jax
import jax.numpy as jnp
from jax import lax

HEADS = 16
HEAD_DIM = 64
D = 1024
FF = 4096
GROUPS = 8
LEN = 1088
SLOTS = 2
SEQS = 64
N_DP = 16
N_FSDP = 2


def draw_counts(key, part):
    key = jax.random.fold_in(key, 7)
    first_key, second_key = jax.random.split(key)
    device_total = N_DP * N_FSDP
    base = jax.random.randint(first_key, (device_total,), 1, SLOTS + 1)
    order = jax.random.permutation(second_key, device_total)
    base = base.at[order[0]].set(SLOTS)
    base = base.at[order[1]].set(1)
    return base.astype(jnp.int32)


def with_ends(values, rng, smallest, largest):
    longest = values.shape.index(max(values.shape))
    spots = []
    for shift in (0, 1):
        where = [jax.random.randint(jax.random.fold_in(rng, axis), (), 0, length) for axis, length in enumerate(values.shape)]
        where[longest] = (where[longest] + shift) % values.shape[longest]
        spots.append(tuple(where))
    return values.at[spots[0]].set(smallest).at[spots[1]].set(largest)


def block_scale(stream_key, shape, shards, smallest, high):
    factor_of = 1.0
    for dim, shards_of in shards:
        draws = jax.random.uniform(jax.random.fold_in(jax.random.fold_in(stream_key, 6), dim), (shards_of,), jnp.float32, smallest / len(shards), high / len(shards))
        factor_of = factor_of * jnp.repeat(jnp.exp(draws), shape[dim] // shards_of).reshape((-1,) + (1,) * (len(shape) - 1 - dim))
    return factor_of


def scatter_about(key, shape, deviation, bound, cuts=(), kind=jnp.bfloat16):
    drawn = deviation * jax.random.normal(key, shape, jnp.float32)
    if cuts:
        drawn = drawn * block_scale(key, shape, cuts, -0.22, 0.18)
    return jnp.clip(drawn, -bound, bound).astype(kind)


def setup_inputs(seed: int = 0) -> dict:
    keys = jax.random.split(jax.random.key(seed), 11)
    tokens = scatter_about(keys[0], (SEQS, LEN, D), 1.0, 6.0, ((0, 32),), jnp.float32)
    cotangent = scatter_about(keys[1], (SEQS, LEN, D), 1.0, 6.0, ((0, 32),), jnp.float32)
    group_ids = with_ends(jax.random.randint(keys[2], (SEQS,), 0, GROUPS), jax.random.fold_in(keys[2], 1), 0, GROUPS - 1).astype(jnp.int32)
    counts = draw_counts(jax.random.fold_in(keys[10], 71), 0)
    w_qkv = scatter_about(keys[4], (D, 3 * D), D ** -0.5, 0.1875, ((0, 2),), jnp.float32)
    w_proj = scatter_about(keys[5], (D, D), (D // 16) ** -0.5, 0.75, ((0, 2),), jnp.float32)
    w_up = scatter_about(keys[6], (D, FF), D ** -0.5, 0.1875, ((0, 2),), jnp.float32)
    w_down = scatter_about(keys[7], (FF, D), FF ** -0.5, 0.09375, ((0, 2),), jnp.float32)
    gains = jnp.clip(1.0 + 0.15 * jax.random.normal(keys[8], (4, D), jnp.float32), 0.25, 1.75)
    table = scatter_about(keys[9], (GROUPS, D), 0.5, 3.0, ((1, 2),), jnp.float32)
    return dict(tokens=tokens, cotangent=cotangent, group_ids=group_ids, counts=counts, w_qkv=w_qkv, w_proj=w_proj, w_up=w_up, w_down=w_down, gains=gains, table=table)


EPSILON = 1e-05
RELAX_ALPHA = 32.0
PRECISE = lax.Precision.HIGHEST

@jax.custom_vjp
def low(v):
    return lax.optimization_barrier(v.astype(jnp.bfloat16)).astype(jnp.float32)

@jax.custom_vjp
def low_back(v):
    return v

def low_keep(v):
    return (low(v), None)

def low_pass(kept, grad):
    return (grad,)

def back_keep(v):
    return (v, None)

def back_low(kept, grad):
    return (low(grad),)
low.defvjp(low_keep, low_pass)
low_back.defvjp(back_keep, back_low)

def norm_rows(hidden_rows):
    centered = hidden_rows - lax.optimization_barrier(jnp.mean(hidden_rows, axis=-1, keepdims=True))
    variance = lax.optimization_barrier(jnp.mean(centered * centered, axis=-1, keepdims=True))
    return centered * lax.rsqrt(variance + EPSILON)

def one_sequence(token_rows, group_id, live_flag, weight_set):
    w_qkv, w_proj, w_up, w_down, gains, table = weight_set
    length = token_rows.shape[0]
    width = HEADS * HEAD_DIM
    start_rows = token_rows + table[group_id][None, :]
    normed_one = low(norm_rows(start_rows) * gains[0])
    packed = low(low_back(jnp.dot(normed_one, w_qkv, precision=PRECISE)))
    queries = packed[:, :width].reshape(length, HEADS, HEAD_DIM)
    key_rows = packed[:, width:2 * width].reshape(length, HEADS, HEAD_DIM)
    value_rows = packed[:, 2 * width:].reshape(length, HEADS, HEAD_DIM)
    scores = low_back(jnp.einsum('qhd,khd->hqk', queries, key_rows, precision=PRECISE))
    relaxed = scores * (1.0 / (RELAX_ALPHA * math.sqrt(HEAD_DIM)))
    position = jnp.arange(length)
    causal = position[:, None] >= position[None, :]
    relaxed = jnp.where(causal[None], relaxed, -1e+30)
    maximum = lax.optimization_barrier(jnp.max(relaxed, axis=-1, keepdims=True))
    expanded = jnp.exp((relaxed - maximum) * RELAX_ALPHA)
    attn_probs = low(expanded / lax.optimization_barrier(jnp.sum(expanded, axis=-1, keepdims=True)))
    joined = jnp.einsum('hqk,khd->qhd', attn_probs, value_rows, precision=PRECISE).reshape(length, width)
    mixture = low(low_back(joined))
    projected = low_back(jnp.dot(mixture, w_proj, precision=PRECISE))
    middle = start_rows + norm_rows(projected) * gains[1]
    normed_two = low(norm_rows(middle) * gains[2])
    up_rows = low_back(jnp.dot(normed_two, w_up, precision=PRECISE))
    activated = low(jax.nn.gelu(up_rows, approximate=False))
    down_rows = low_back(jnp.dot(activated, w_down, precision=PRECISE))
    return (middle + norm_rows(down_rows) * gains[3]) * live_flag

def reference(tokens, cotangent, group_ids, counts, w_qkv, w_proj, w_up, w_down, gains, table):
    slot_index = jnp.arange(tokens.shape[0])
    live = (slot_index % SLOTS < counts[slot_index // SLOTS]).astype(tokens.dtype)
    block_fn = jax.checkpoint(one_sequence)

    def forward(token_all, weight_a, weight_b, weight_c, weight_d, gain_all, table_all):
        weight_set = (low(weight_a), low(weight_b), low(weight_c), low(weight_d), low(gain_all), low(table_all))
        return lax.map(lambda slot_item: block_fn(slot_item[0], slot_item[1], slot_item[2], weight_set), (token_all, group_ids, live))
    output, pullback = jax.vjp(forward, tokens, w_qkv, w_proj, w_up, w_down, gains, table)
    grads = pullback(cotangent)
    return (output, grads[0], grads[1], grads[2], grads[3], grads[4], grads[5], grads[6])
```

```python
import math

import jax
import jax.numpy as jnp
from jax import lax
from jax.experimental import pallas as pl
from jax.experimental.pallas import tpu as pltpu
from jax.sharding import PartitionSpec as P

HEAD_DIM = 64
LANES = 128
EPSILON = 1e-05
NEG = -1e30
ATTN_ROWS = 256
VMEM_BYTES = 60 * 1024 * 1024


def dot(a, b, a_dim, b_dim):
    return lax.dot_general(a, b, (((a_dim,), (b_dim,)), ((), ())), preferred_element_type=jnp.float32)


def params(*semantics):
    return pltpu.CompilerParams(vmem_limit_bytes=VMEM_BYTES)


def cost(micros):
    return pl.CostEstimate(flops=int(micros * 1e9), bytes_accessed=int(micros * 1e6), transcendentals=0)


def row_block(length, most):
    return max(b for b in range(16, most + 1, 16) if length % b == 0)


def normed(rows):
    centered = rows - jnp.mean(rows, axis=-1, keepdims=True)
    inv_std = lax.rsqrt(jnp.mean(centered * centered, axis=-1, keepdims=True) + EPSILON)
    return centered * inv_std, inv_std


def norm_back(gradient, unit, inv_std, gain):
    grad_unit = gradient * gain
    first = jnp.mean(grad_unit, axis=-1, keepdims=True)
    second = jnp.mean(grad_unit * unit, axis=-1, keepdims=True)
    return inv_std * (grad_unit - first - unit * second)


def gelu_parts(u):
    cdf = 0.5 + 0.5 * lax.erf(u * math.sqrt(0.5))
    return u * cdf, cdf + u * jnp.exp(-0.5 * u * u) * (1.0 / math.sqrt(2.0 * math.pi))


def staged(jobs, one, two, three):
    n, firsts, seconds = len(jobs), {}, {}
    for i in range(n + 2):
        if i < n:
            firsts[i] = one(jobs[i])
        if i >= 2:
            three(jobs[i - 2], seconds.pop(i - 2))
        if 1 <= i <= n:
            seconds[i - 1] = two(jobs[i - 1], firsts.pop(i - 1))


def spans(length):
    return [(s, min(s + ATTN_ROWS, length)) for s in range(0, length, ATTN_ROWS)]


class Weights:
    def __init__(self, matrices):
        self.refs = [part[0] for parts, _ in matrices for part in parts]
        self.parts = [[part[1:] for part in parts] for parts, _ in matrices]
        self.shapes = [shape for _, shape in matrices]
        self.starts = jnp.stack([jnp.asarray(part[1], jnp.int32) for parts, _ in matrices for part in parts])
        self.in_specs = [pl.BlockSpec(memory_space=pl.ANY)] * len(self.refs)
        self.scratch = [pltpu.VMEM(shape, jnp.bfloat16) for shape in self.shapes]
        n_copies = sum(len(part[1]) if len(part) > 1 else 1 for parts in self.parts for part in parts)
        self.scratch.append(pltpu.SemaphoreType.DMA((n_copies,)))

    def copies(self, starts_ref, refs, scratch):
        lists, at, n = [], 0, 0
        for parts, whole in zip(self.parts, scratch[:-1]):
            mine = []
            for part in parts:
                rows = pl.ds(pl.multiple_of(starts_ref[at], 16), refs[at].shape[-2])
                pairs = [(refs[at], whole.at[..., rows, :])]
                if len(part) > 1:
                    pairs = [(refs[at].at[:, lo:hi], whole.at[i, rows, :]) for i, (lo, hi) in enumerate(part[1])]
                for source, target in pairs:
                    mine.append(pltpu.make_async_copy(source, target, scratch[-1].at[n]))
                    n += 1
                at += 1
            lists.append(mine)
        return lists


def run_all(copies, method):
    for copy in copies:
        getattr(copy, method)()


def project_in(tokens, added, gain, weight):
    slots, length, width = tokens.shape
    part = weight[1][2]
    block = row_block(length, 544)
    held = Weights([weight])
    n_held = len(held.refs)

    def kernel(starts_ref, x_ref, e_ref, g_ref, *rest):
        refs, (a_ref, out_ref), scratch = rest[:n_held], rest[n_held : n_held + 2], rest[n_held + 2 :]
        first = (pl.program_id(0) == 0) & (pl.program_id(1) == 0)
        copies = held.copies(starts_ref, refs, scratch)[0]

        @pl.when(first)
        def _():
            run_all(copies, "start")

        a = (normed(x_ref[0] + e_ref[0])[0] * g_ref[...]).astype(jnp.bfloat16)
        a_ref[0] = a

        @pl.when(first)
        def _():
            run_all(copies, "wait")

        for i in range(3):
            out_ref[i, 0] = dot(a, scratch[0][i], 1, 0).astype(jnp.bfloat16)

    rows = pl.BlockSpec((1, block, width), lambda s, i, _: (s, i, 0))
    return pl.pallas_call(
        kernel,
        grid_spec=pltpu.PrefetchScalarGridSpec(
            num_scalar_prefetch=1,
            grid=(slots, length // block),
            in_specs=[
                rows,
                pl.BlockSpec((1, 1, width), lambda s, i, _: (s, 0, 0)),
                pl.BlockSpec((1, width), lambda s, i, _: (0, 0)),
            ]
            + held.in_specs,
            out_specs=[rows, pl.BlockSpec((3, 1, block, part), lambda s, i, _: (0, s, i, 0))],
            scratch_shapes=held.scratch,
        ),
        out_shape=[
            jax.ShapeDtypeStruct(tokens.shape, jnp.bfloat16),
            jax.ShapeDtypeStruct((3, slots, length, part), jnp.bfloat16),
        ],
        compiler_params=params(),
        cost_estimate=cost(14),
        name="project_in",
    )(held.starts, tokens, added, gain, *held.refs)


def causal(scores, keys_first):
    q = lax.broadcasted_iota(jnp.int32, scores.shape, 1 if keys_first else 0)
    k = lax.broadcasted_iota(jnp.int32, scores.shape, 0 if keys_first else 1)
    return q >= k


def attn_fwd_kernel(x_ref, o_ref, l_ref):
    length = x_ref.shape[2]
    first = lax.broadcasted_iota(jnp.int32, (1, LANES), 1) < HEAD_DIM
    jobs = [(lo, hi, h) for lo, hi in spans(length) for h in range(2)]
    outs = {}

    def scores(job):
        lo, hi, h = job
        q = x_ref[0, 0, lo:hi, :] * (1.0 / math.sqrt(HEAD_DIM))
        q = jnp.where(first if h == 0 else ~first, q, 0).astype(jnp.bfloat16)
        near = dot(q, x_ref[1, 0, lo:hi, :], 1, 1)
        near = jnp.where(causal(near, False), near, NEG)
        return near, dot(q, x_ref[1, 0, 0:lo, :], 1, 1) if lo else None

    def weights(job, both):
        near, far = both
        top = jnp.max(near, axis=1, keepdims=True)
        if far is not None:
            top = jnp.maximum(top, jnp.max(far, axis=1, keepdims=True))
        near = jnp.exp(near - top)
        total = jnp.sum(near, axis=1, keepdims=True)
        if far is not None:
            far = jnp.exp(far - top)
            total = total + jnp.sum(far, axis=1, keepdims=True)
            far = far.astype(jnp.bfloat16)
        return near.astype(jnp.bfloat16), far, top, total

    def mix(job, parts):
        lo, hi, h = job
        near, far, top, total = parts
        o = dot(near, x_ref[2, 0, lo:hi, :], 1, 0)
        if far is not None:
            o = o + dot(far, x_ref[2, 0, 0:lo, :], 1, 0)
        outs[h] = o / total
        log_total = jnp.broadcast_to(top + jnp.log(total), (hi - lo, LANES))
        l_ref[0, 0, h : h + 1, lo:hi] = jnp.transpose(log_total)[0:1, :]
        if h == 1:
            o_ref[0, lo:hi, :] = jnp.where(first, outs[0], outs[1]).astype(jnp.bfloat16)

    staged(jobs, scores, weights, mix)


def attn_fwd(qkv, start, count, first_pair, width, before=None):
    _, slots, length, _ = qkv.shape
    place = first_pair + start
    n_before = 0 if before is None else 2

    def kernel(x_ref, *rest):
        attn_fwd_kernel(x_ref, *rest[n_before:])

    return pl.pallas_call(
        kernel,
        grid=(slots, count),
        in_specs=[pl.BlockSpec((3, 1, length, LANES), lambda s, p: (0, s, 0, start + p))]
        + [pl.BlockSpec(memory_space=pl.ANY)] * n_before,
        out_specs=[
            pl.BlockSpec((1, length, LANES), lambda s, p: (s, 0, place + p)),
            pl.BlockSpec((1, 1, 2, length), lambda s, p: (s, place + p, 0, 0)),
        ],
        out_shape=[
            jax.ShapeDtypeStruct((slots, length, width), jnp.bfloat16),
            jax.ShapeDtypeStruct((slots, width // LANES, 2, length), jnp.float32),
        ],
        input_output_aliases={1 + i: i for i in range(n_before)},
        compiler_params=params(),
        cost_estimate=cost(8 * count),
        name="attn_fwd",
    )(qkv, *(before or ()))


def attn_bwd_kernel(x_ref, o_ref, do_ref, l_ref, d_ref, dqt_ref):
    length = x_ref.shape[2]
    scale = 1.0 / math.sqrt(HEAD_DIM)
    first = lax.broadcasted_iota(jnp.int32, (1, LANES), 1) < HEAD_DIM
    q = x_ref[0, 0] * scale
    do = do_ref[0]
    prod = jnp.transpose(do.astype(jnp.float32) * o_ref[0].astype(jnp.float32))
    deltas = [jnp.sum(prod[:HEAD_DIM], axis=0, keepdims=True), jnp.sum(prod[HEAD_DIM:], axis=0, keepdims=True)]
    dqt_ref[...] = jnp.zeros_like(dqt_ref)
    jobs = []
    for lo, hi in spans(length):
        for h in range(2):
            jobs.append((lo, hi, h, lo, hi))
            if hi < length:
                jobs.append((lo, hi, h, hi, length))
    sums = {}

    def scores(job):
        lo, hi, h, a, b = job
        mine = lambda v: jnp.where(first if h == 0 else ~first, v, 0).astype(jnp.bfloat16)
        return dot(mine(x_ref[1, 0, lo:hi, :]), q[a:b], 1, 1), dot(mine(x_ref[2, 0, lo:hi, :]), do[a:b], 1, 1)

    def weights(job, both):
        lo, hi, h, a, b = job
        p = jnp.exp(both[0] - l_ref[0, 0, h : h + 1, a:b])
        if a == lo:
            p = jnp.where(causal(p, True), p, 0.0)
        return p.astype(jnp.bfloat16), (p * (both[1] - deltas[h][:, a:b])).astype(jnp.bfloat16)

    def collect(job, parts):
        lo, hi, h, a, b = job
        p, ds = parts
        dv, dk = dot(p, do[a:b], 1, 0), dot(ds, q[a:b], 1, 0)
        sums[h] = (dk, dv) if a == lo else (sums[h][0] + dk, sums[h][1] + dv)
        lanes = slice(h * HEAD_DIM, (h + 1) * HEAD_DIM)
        kt = jnp.transpose(x_ref[1, 0, lo:hi, :].astype(jnp.float32)).astype(jnp.bfloat16)
        dqt_ref[lanes, a:b] += dot(kt[lanes], ds, 1, 0)
        if h == 1 and b == length:
            for i in range(2):
                d_ref[1 + i, 0, lo:hi, :] = jnp.where(first, sums[0][i], sums[1][i]).astype(jnp.bfloat16)

    staged(jobs, scores, weights, collect)
    d_ref[0, 0] = (jnp.transpose(dqt_ref[...]) * scale).astype(jnp.bfloat16)


def attn_bwd(qkv, mixture, grad_mix, log_totals, start, count, first_pair):
    _, slots, length, _ = qkv.shape
    place = first_pair + start
    triple = pl.BlockSpec((3, 1, length, LANES), lambda s, p: (0, s, 0, start + p))
    single = pl.BlockSpec((1, length, LANES), lambda s, p: (s, 0, place + p))
    return pl.pallas_call(
        attn_bwd_kernel,
        grid=(slots, count),
        in_specs=[triple, single, single, pl.BlockSpec((1, 1, 2, length), lambda s, p: (s, place + p, 0, 0))],
        out_specs=pl.BlockSpec((3, 1, length, LANES), lambda s, p: (0, s, 0, p)),
        out_shape=jax.ShapeDtypeStruct((3, slots, length, count * LANES), jnp.bfloat16),
        scratch_shapes=[pltpu.VMEM((LANES, length), jnp.float32)],
        compiler_params=params(),
        cost_estimate=cost(6 * count),
        name="attn_bwd",
    )(qkv, mixture, grad_mix, log_totals)


def token_specs(shape, block):
    slots, length, width = shape
    rows = pl.BlockSpec((1, block, width), lambda s, i, *_: (s, i, 0))
    per_slot = lambda n: pl.BlockSpec((1, n, width), lambda s, i, *_: (s, 0, 0))
    whole = lambda v: pl.BlockSpec(v.shape, lambda s, i, *_: (0,) * v.ndim)
    return rows, per_slot, whole


def up_and_down(live, mixture, tokens, cotangent, added, gains, w_proj, w_up, w_down):
    slots, length, width = tokens.shape
    hidden = w_up[1][1]
    block = row_block(length, 272)
    chunk = min(512, hidden)
    held = Weights([w_proj, w_up, w_down])
    n_held = len(held.refs)

    def kernel(starts_ref, live_ref, o_ref, x_ref, c_ref, e_ref, g_ref, *rest):
        refs = rest[:n_held]
        a_ref, f_ref, slope_ref, dm_ref, z_ref, h_ref, out_ref, sum_ref = rest[n_held : n_held + 8]
        wp, wu, wd = rest[n_held + 8 : n_held + 11]

        @pl.when((pl.program_id(0) == 0) & (pl.program_id(1) == 0))
        def _():
            copies = held.copies(starts_ref, refs, rest[n_held + 8 : n_held + 12])
            for some in copies:
                run_all(some, "start")
            for some in copies:
                run_all(some, "wait")

        @pl.when(pl.program_id(1) == 0)
        def _():
            sum_ref[...] = jnp.zeros_like(sum_ref)

        alive = live_ref[pl.program_id(0)].astype(jnp.float32)
        z = dot(o_ref[0], wp[...], 1, 0)
        z_ref[0] = z
        h1 = x_ref[0] + e_ref[0] + normed(z)[0] * g_ref[1:2]
        h_ref[0] = h1
        a = (normed(h1)[0] * g_ref[2:3]).astype(jnp.bfloat16)
        a_ref[0] = a
        m = []

        def activate(cols, u):
            f, slope = gelu_parts(u)
            f_ref[0, :, cols] = f.astype(jnp.bfloat16)
            slope_ref[0, :, cols] = slope.astype(jnp.bfloat16)
            return f.astype(jnp.bfloat16)

        def lower(cols, f):
            more = dot(f, wd[cols, :], 1, 0)
            m[:] = [m[0] + more] if m else [more]

        cols = [slice(j, j + chunk) for j in range(0, hidden, chunk)]
        staged(cols, lambda c: dot(a, wu[:, c], 1, 0), activate, lower)
        unit_m, inv_m = normed(m[0])
        out_ref[0] = alive * (h1 + unit_m * g_ref[3:4])
        dy = alive * c_ref[0]
        dm_ref[0] = norm_back(dy, unit_m, inv_m, g_ref[3:4]).astype(jnp.bfloat16)
        sum_ref[0, 0:1] += jnp.sum(dy * unit_m, axis=0, keepdims=True)

    rows, per_slot, whole = token_specs(tokens.shape, block)
    wide = pl.BlockSpec((1, block, hidden), lambda s, i, *_: (s, i, 0))
    low = jax.ShapeDtypeStruct(tokens.shape, jnp.bfloat16)
    low_wide = jax.ShapeDtypeStruct((slots, length, hidden), jnp.bfloat16)
    full = jax.ShapeDtypeStruct(tokens.shape, jnp.float32)
    return pl.pallas_call(
        kernel,
        grid_spec=pltpu.PrefetchScalarGridSpec(
            num_scalar_prefetch=2,
            grid=(slots, length // block),
            in_specs=[rows, rows, rows, per_slot(1), whole(gains)] + held.in_specs,
            out_specs=[rows, wide, wide, rows, rows, rows, rows, per_slot(8)],
            scratch_shapes=held.scratch,
        ),
        out_shape=[low, low_wide, low_wide, low, full, full, full, jax.ShapeDtypeStruct((slots, 8, width), jnp.float32)],
        compiler_params=params(),
        cost_estimate=cost(80),
        name="up_and_down",
    )(held.starts, live, mixture, tokens, cotangent, added, gains, *held.refs)


def back_to_hidden(dm, slope, w_down):
    slots, length, width = dm.shape
    hidden = slope.shape[-1]
    block = row_block(length, 544)
    chunk = min(512, hidden)
    held = Weights([w_down])
    n_held = len(held.refs)

    def kernel(starts_ref, dm_ref, slope_ref, *rest):
        refs, du_ref, scratch = rest[:n_held], rest[n_held], rest[n_held + 1 :]

        @pl.when((pl.program_id(0) == 0) & (pl.program_id(1) == 0))
        def _():
            copies = held.copies(starts_ref, refs, scratch)[0]
            run_all(copies, "start")
            run_all(copies, "wait")

        dm_block = dm_ref[0]
        for j in range(0, hidden, chunk):
            df = dot(dm_block, scratch[0][j : j + chunk, :], 1, 1)
            du_ref[0, :, j : j + chunk] = (df * slope_ref[0, :, j : j + chunk].astype(jnp.float32)).astype(jnp.bfloat16)

    rows, _, _ = token_specs(dm.shape, block)
    wide = pl.BlockSpec((1, block, hidden), lambda s, i, *_: (s, i, 0))
    return pl.pallas_call(
        kernel,
        grid_spec=pltpu.PrefetchScalarGridSpec(
            num_scalar_prefetch=1,
            grid=(slots, length // block),
            in_specs=[rows, wide] + held.in_specs,
            out_specs=wide,
            scratch_shapes=held.scratch,
        ),
        out_shape=jax.ShapeDtypeStruct(slope.shape, jnp.bfloat16),
        compiler_params=params(),
        cost_estimate=cost(25),
        name="back_to_hidden",
    )(held.starts, dm, slope, *held.refs)


def back_to_mixture(live, du, h1, z, cotangent, gains, w_proj, w_up):
    slots, length, width = h1.shape
    hidden = du.shape[-1]
    block = row_block(length, 272)
    held = Weights([w_up, w_proj])
    n_held = len(held.refs)

    def kernel(starts_ref, live_ref, du_ref, h_ref, z_ref, c_ref, g_ref, *rest):
        refs = rest[:n_held]
        dz_ref, do_ref, dh_ref, sum_ref = rest[n_held : n_held + 4]
        wu, wp = rest[n_held + 4 : n_held + 6]

        @pl.when((pl.program_id(0) == 0) & (pl.program_id(1) == 0))
        def _():
            copies = held.copies(starts_ref, refs, rest[n_held + 4 : n_held + 7])
            for some in copies:
                run_all(some, "start")
            for some in copies:
                run_all(some, "wait")

        @pl.when(pl.program_id(1) == 0)
        def _():
            sum_ref[...] = jnp.zeros_like(sum_ref)

        alive = live_ref[pl.program_id(0)].astype(jnp.float32)
        da = dot(du_ref[0], wu[...], 1, 1)
        unit_h, inv_h = normed(h_ref[0])
        unit_z, inv_z = normed(z_ref[0])
        dh1 = alive * c_ref[0] + norm_back(da, unit_h, inv_h, g_ref[2:3])
        dh_ref[0] = dh1
        dz = norm_back(dh1, unit_z, inv_z, g_ref[1:2]).astype(jnp.bfloat16)
        dz_ref[0] = dz
        do_ref[0] = dot(dz, wp[...], 1, 1).astype(jnp.bfloat16)
        sum_ref[0, 0:1] += jnp.sum(dh1 * unit_z, axis=0, keepdims=True)
        sum_ref[0, 1:2] += jnp.sum(da * unit_h, axis=0, keepdims=True)

    rows, per_slot, whole = token_specs(h1.shape, block)
    wide = pl.BlockSpec((1, block, hidden), lambda s, i, *_: (s, i, 0))
    low = jax.ShapeDtypeStruct(h1.shape, jnp.bfloat16)
    return pl.pallas_call(
        kernel,
        grid_spec=pltpu.PrefetchScalarGridSpec(
            num_scalar_prefetch=2,
            grid=(slots, length // block),
            in_specs=[wide, rows, rows, rows, whole(gains)] + held.in_specs,
            out_specs=[rows, rows, rows, per_slot(8)],
            scratch_shapes=held.scratch,
        ),
        out_shape=[
            low,
            low,
            jax.ShapeDtypeStruct(h1.shape, jnp.float32),
            jax.ShapeDtypeStruct((slots, 8, width), jnp.float32),
        ],
        compiler_params=params(),
        cost_estimate=cost(40),
        name="back_to_mixture",
    )(held.starts, live, du, h1, z, cotangent, gains, *held.refs)


def project_back(slot, groups, tokens, grad_middle, added, gain, weights):
    _, length, width = tokens.shape
    block = row_block(length, 272)
    held = Weights(weights)
    per_weight = len(groups) // len(weights)
    n_held = len(held.refs)

    n_groups, part = len(groups), groups[0].shape[-1]

    def kernel(starts_ref, *refs_in):
        d_refs, (x_ref, h_ref, e_ref, g_ref), rest = refs_in[:n_groups], refs_in[n_groups : n_groups + 4], refs_in[n_groups + 4 :]
        refs, (out_ref, sum_ref), scratch = rest[:n_held], rest[n_held : n_held + 2], rest[n_held + 2 :]
        first = pl.program_id(0) == 0
        copies = sum(held.copies(starts_ref, refs, scratch), [])

        @pl.when(first)
        def _():
            run_all(copies, "start")

        unit, inv_std = normed(x_ref[0] + e_ref[0])

        @pl.when(first)
        def _():
            run_all(copies, "wait")

        da = None
        for w in range(len(weights)):
            mine = d_refs[w * per_weight : (w + 1) * per_weight]
            for i in range(3):
                more = dot(jnp.concatenate([ref[i, 0] for ref in mine], axis=1), scratch[w][i], 1, 1)
                da = more if da is None else da + more
        dh = h_ref[0] + norm_back(da, unit, inv_std, g_ref[...])
        out_ref[0] = dh

        @pl.when(pl.program_id(0) == 0)
        def _():
            sum_ref[...] = jnp.zeros_like(sum_ref)

        sum_ref[0, 0:1] += jnp.sum(da * unit, axis=0, keepdims=True)
        sum_ref[0, 1:2] += jnp.sum(dh, axis=0, keepdims=True)

    rows = pl.BlockSpec((1, block, width), lambda i, _: (slot, i, 0))
    return pl.pallas_call(
        kernel,
        grid_spec=pltpu.PrefetchScalarGridSpec(
            num_scalar_prefetch=1,
            grid=(length // block,),
            in_specs=[pl.BlockSpec((3, 1, block, part), lambda i, _: (0, slot, i, 0))] * n_groups
            + [
                rows,
                rows,
                pl.BlockSpec((1, 1, width), lambda i, _: (slot, 0, 0)),
                pl.BlockSpec((1, width), lambda i, _: (0, 0)),
            ]
            + held.in_specs,
            out_specs=[
                pl.BlockSpec((1, block, width), lambda i, _: (0, i, 0)),
                pl.BlockSpec((1, 8, width), lambda i, _: (0, 0, 0)),
            ],
            scratch_shapes=held.scratch,
        ),
        out_shape=[
            jax.ShapeDtypeStruct((1,) + tokens.shape[1:], jnp.float32),
            jax.ShapeDtypeStruct((1, 8, width), jnp.float32),
        ],
        compiler_params=params(),
        cost_estimate=cost(15),
        name="project_back",
    )(held.starts, *groups, tokens, grad_middle, added, gain, *held.refs)


def grad_blocks(order, left, right, received=None):
    rows, depth = left.shape[0], left.shape[1] // 4
    tall = min(depth, 512)
    per_block = depth // tall
    stacked = isinstance(right, list)
    if stacked:
        count, slab = right[0].shape[0], sum(r.shape[-1] for r in right)
        right_specs = [pl.BlockSpec((1, rows, r.shape[-1]), lambda r, k, j, order: (j, 0, 0)) for r in right]
    else:
        slab = min(1024, right.shape[1])
        count = right.shape[1] // slab
        right_specs = [pl.BlockSpec((rows, slab), lambda r, k, j, order: (0, j))]
        right = [right]
    n_right = len(right)

    def kernel(order_ref, a_ref, *rest):
        if stacked:
            right_block = jnp.concatenate([ref[0] for ref in rest[:n_right]], axis=1)
        else:
            right_block = rest[0][...]
        outs = rest[n_right:]
        total = dot(a_ref[...], right_block, 0, 0)
        if received is None:
            outs[0][0, 0] = total.astype(jnp.bfloat16)
            return
        total = (total + outs[0][0, 0].astype(jnp.float32)).astype(jnp.bfloat16)

        @pl.when(pl.program_id(0) == 0)
        def _():
            outs[1][0] = total

        @pl.when(pl.program_id(0) == 1)
        def _():
            outs[2][0] = total

    both = pl.BlockSpec((1, 1, tall, slab), lambda r, k, j, order: (r, j, k, 0))
    sent = pl.BlockSpec((1, tall, slab), lambda r, k, j, order: (jnp.where(r == 0, j, count - 1), jnp.where(r == 0, k, per_block - 1), 0))
    kept = pl.BlockSpec((1, tall, slab), lambda r, k, j, order: (jnp.where(r == 0, 0, j), jnp.where(r == 0, 0, k), 0))
    more = [] if received is None else [received]
    shape = (count, depth, slab)
    return pl.pallas_call(
        kernel,
        grid_spec=pltpu.PrefetchScalarGridSpec(
            num_scalar_prefetch=1,
            grid=(2, per_block, count),
            in_specs=[pl.BlockSpec((rows, tall), lambda r, k, j, order: (0, order[r] * per_block + k))]
            + right_specs
            + [both] * len(more),
            out_specs=[sent, kept] if more else both,
        ),
        out_shape=[jax.ShapeDtypeStruct(shape, jnp.bfloat16)] * 2 if more else jax.ShapeDtypeStruct((2,) + shape, jnp.bfloat16),
        compiler_params=params(),
        cost_estimate=cost(rows * left.shape[1] * slab * count // 10**9),
        name="grad_blocks",
    )(order, left, *right, *more)


def after(value, *earlier):
    return lax.optimization_barrier((value,) + earlier)[0]


def swap(value, axis, bit):
    size = lax.axis_size(axis)
    return lax.ppermute(value, axis, [(i, i ^ (1 << bit)) for i in range(size)])


def bit_of(axis, bit):
    return (lax.axis_index(axis) >> bit) & 1


def bits_of(axis):
    return range(lax.axis_size(axis).bit_length() - 1)


def pick(value, index):
    return lax.dynamic_index_in_dim(value, index, 0, keepdims=False)


def paired():
    return lax.axis_size("fsdp") == 2 and lax.axis_size("dp") % 2 == 0


def slot(before, ends=(), starts=()):
    before = tuple(before)
    if not paired():
        for e in ends:
            e.take()
        return before
    if ends:
        arrived = lax.optimization_barrier(tuple(e.received for e in ends) + before)
        for e, value in zip(ends, arrived):
            e.received = value
            e.take()
        before = arrived[len(ends) :]
    if starts:
        leaving = lax.optimization_barrier(tuple(e.sent for e in starts) + before)
        for e, value in zip(starts, leaving):
            e.send(value)
        before = leaving
    return before


class Gather:
    def __init__(self, low, ranges=None):
        self.low, self.ranges = low, ranges
        self.size, wide = low.shape
        whole = self.size * lax.axis_size("fsdp")
        self.shape = (whole, wide) if ranges is None else (len(ranges), whole, ranges[0][1] - ranges[0][0])
        self.crossed = None
        if paired():
            half = self.size // 2
            mine = lambda lo, hi: lax.dynamic_slice(low, (bit_of("dp", 0) * half, lo), (half, hi - lo))
            self.sent = mine(0, wide) if ranges is None else jnp.stack([mine(lo, hi) for lo, hi in ranges])
        else:
            self.sent = low

    def send(self, value):
        self.received = swap(value, "fsdp" if self.crossed is None else "dp", 0)

    def take(self):
        if not paired():
            return
        if self.crossed is None:
            self.crossed = self.sent = self.received
        else:
            self.beside = self.received

    def parts(self):
        ranges = () if self.ranges is None else (self.ranges,)
        if not paired():
            return [(lax.all_gather(self.low, "fsdp", axis=0, tiled=True), 0) + ranges], self.shape
        size, c, x = self.size, bit_of("dp", 0), lax.axis_index("fsdp")
        base = (1 - x) * size
        own = (self.low, x * size) + ranges
        return [own, (self.crossed, base + c * (size // 2)), (self.beside, base + (1 - c) * (size // 2))], self.shape


class WideGather:
    def __init__(self, low):
        self.low = low
        self.shape = (low.shape[0] * lax.axis_size("fsdp"), low.shape[1])
        self.crossed = None
        self.sent = low
        if paired():
            n_dp = lax.axis_size("dp")
            self.sent = pick(low.reshape(n_dp, low.shape[0] // n_dp, low.shape[1]), lax.axis_index("dp"))

    def send(self, value):
        if self.crossed is None:
            self.received = swap(value, "fsdp", 0)
        else:
            self.other = lax.all_gather(value, "dp", axis=0, tiled=True)

    def take(self):
        if paired():
            self.crossed = self.sent = self.received

    def parts(self):
        if not paired():
            return [(lax.all_gather(self.low, "fsdp", axis=0, tiled=True), 0)], self.shape
        size, x = self.low.shape[0], lax.axis_index("fsdp")
        return [(self.low, x * size), (self.other, (1 - x) * size)], self.shape


class Columns:
    def __init__(self, low):
        self.low = self.sent = low

    def send(self, value):
        self.received = swap(value, "fsdp", 0)

    def take(self):
        if not paired():
            self.whole = lax.all_gather(self.low, "fsdp", axis=1, tiled=True)
            return
        first = lax.axis_index("fsdp") == 0
        self.whole = jnp.concatenate(
            [jnp.where(first, self.low, self.received), jnp.where(first, self.received, self.low)], axis=1
        )


class SmallSum:
    def __init__(self, value):
        self.value, self.bits = value, None
        if paired():
            halves = value.reshape(value.shape[0], 2, -1)
            x = lax.axis_index("fsdp")
            self.value = lax.dynamic_index_in_dim(halves, x, 1, keepdims=False)
            self.sent = lax.dynamic_index_in_dim(halves, 1 - x, 1, keepdims=False)

    def send(self, value):
        if self.bits is None:
            self.bits = list(bits_of("dp"))
            self.received = swap(value, "fsdp", 0)
        else:
            self.received = swap(value, "dp", self.bits.pop(0))

    def take(self):
        if paired():
            self.value = self.sent = self.value + self.received

    def result(self):
        if paired():
            return self.value
        return lax.psum(lax.psum_scatter(self.value, "fsdp", scatter_dimension=1, tiled=True), "dp")


def assemble(pieces):
    count, rows, wide = pieces[0][0].shape
    n_pieces = len(pieces)

    def kernel(c_ref, *refs):
        out_ref = refs[-1]
        for p in range(n_pieces):

            @pl.when(pl.program_id(1) == p)
            def _():
                for i, ref in enumerate(refs[2 * p : 2 * p + 2]):
                    half = c_ref[0] if i == 0 else 1 - c_ref[0]
                    out_ref[pl.ds(pl.multiple_of(half * rows, rows), rows), :] = ref[0].astype(jnp.float32)

    return pl.pallas_call(
        kernel,
        grid_spec=pltpu.PrefetchScalarGridSpec(
            num_scalar_prefetch=1,
            grid=(count, n_pieces),
            in_specs=[pl.BlockSpec((1, rows, wide), lambda i, p, c: (i, 0, 0))] * (2 * n_pieces),
            out_specs=pl.BlockSpec((2 * rows, wide), lambda i, p, c: (0, i * n_pieces + p)),
        ),
        out_shape=jax.ShapeDtypeStruct((2 * rows, count * n_pieces * wide), jnp.float32),
        compiler_params=params(),
        cost_estimate=cost(4),
        name="assemble",
    )(bit_of("dp", 0).astype(jnp.int32).reshape(1), *[v for piece in pieces for v in piece])


def in_rows(whole):
    n, count, rows, wide = whole.shape
    n_bits = n.bit_length() - 1
    step = min(wide, 512)

    def place(i):
        return sum(((i >> (n_bits - 1 - b)) & 1) << b for b in range(n_bits))

    def kernel(in_ref, out_ref):
        for i in range(n):
            out_ref[place(i) * rows : (place(i) + 1) * rows, :] = in_ref[i, 0].astype(jnp.float32)

    return pl.pallas_call(
        kernel,
        grid=(count, wide // step),
        in_specs=[pl.BlockSpec((n, 1, rows, step), lambda s, j: (0, s, 0, j))],
        out_specs=pl.BlockSpec((n * rows, step), lambda s, j: (0, s * (wide // step) + j)),
        out_shape=jax.ShapeDtypeStruct((n * rows, count * wide), jnp.float32),
        compiler_params=params(),
        name="in_rows",
    )(whole)


class GradSum:
    def __init__(self, left, right, spread=False):
        self.left, self.right, self.spread = left, right, spread
        self.state = "send"
        if paired():
            self.bits = list(bits_of("dp"))[1:]

    def part(self, before):
        if not paired():
            if self.state == "send":
                right = self.right
                if isinstance(right, list):
                    right = jnp.concatenate([r[i] for i in range(3) for r in right], axis=1)
                low = dot(self.left, right, 0, 0).astype(jnp.bfloat16)
                piece = lax.psum_scatter(low, ("fsdp", "dp"), scatter_dimension=0, tiled=True)
                self.total = lax.all_gather(piece, "dp", axis=0, tiled=True).astype(jnp.float32)
                self.state = "keep"
            return before
        c, x = bit_of("dp", 0), lax.axis_index("fsdp")
        left = after(self.left, *before)
        if self.state == "send":
            order = jnp.stack([(1 - x) * 2 + 1 - c, x * 2 + 1 - c]).astype(jnp.int32)
            self.sent = grad_blocks(order, left, self.right)
        else:
            order = jnp.stack([(1 - x) * 2 + c, x * 2 + c]).astype(jnp.int32)
            self.sent, self.kept = grad_blocks(order, left, self.right, self.received)
        return (self.sent,)

    def send(self, value):
        if self.state == "send":
            self.received = swap(value, "dp", 0)
        elif self.state == "keep":
            self.received = swap(value, "fsdp", 0)
        elif self.state == "halve":
            self.received = swap(value, "dp", self.bit)
        elif self.spread:
            self.whole = lax.all_gather(value, "dp", axis=0, tiled=False)
        else:
            self.received = swap(value, "dp", self.bit)

    def take(self):
        if not paired():
            return
        if self.state == "send":
            self.state = "keep"
        elif self.state in ("keep", "halve"):
            if self.bits:
                self.state, self.bit = "halve", self.bits.pop(0)
                b = bit_of("dp", self.bit)
                slabs, rows, wide = self.kept.shape
                kept, received = (v.reshape(slabs, 2, rows // 2, wide) for v in (self.kept, self.received))
                part = lambda v, i: lax.dynamic_index_in_dim(v, i, 1, keepdims=False).astype(jnp.float32)
                self.sent = (part(kept, 1 - b) + part(received, 1 - b)).astype(jnp.bfloat16)
                self.kept = (part(kept, b) + part(received, b)).astype(jnp.bfloat16)
            else:
                self.kept = self.sent = (self.kept.astype(jnp.float32) + self.received.astype(jnp.float32)).astype(jnp.bfloat16)
                self.state, self.bits = "join", list(bits_of("dp"))
                self.bit = self.bits.pop()
        elif self.bits:
            self.kept = self.sent = in_order(self.kept, self.received, bit_of("dp", self.bit))
            self.bit = self.bits.pop()
        else:
            self.state = "done"

    def result(self, *earlier):
        if not paired():
            return self.total
        if self.spread:
            return in_rows(after(self.whole, *earlier))
        return assemble([(self.kept, self.received)])


def in_order(mine, other, bit):
    return jnp.where(bit == 0, jnp.concatenate([mine, other], axis=1), jnp.concatenate([other, mine], axis=1))


def local(tokens, cotangent, group_ids, counts, w_qkv, w_proj, w_up, w_down, gains, table):
    slots, length, width = tokens.shape
    rows = slots * length
    flat = lambda v: v.reshape(v.shape[:-3] + (rows, v.shape[-1]))
    pairs = width // LANES
    n_groups = 2
    group_pairs = pairs // n_groups
    half = group_pairs // 2
    part = width // n_groups
    small = Columns(jnp.concatenate([gains, table], axis=0).astype(jnp.bfloat16))
    low_qkv = w_qkv.astype(jnp.bfloat16)
    get_qkv = [
        Gather(low_qkv, [(i * width + j * part, i * width + (j + 1) * part) for i in range(3)]) for j in range(n_groups)
    ]
    t = slot((), starts=[small, get_qkv[0]])
    get_down = WideGather(after(w_down, *t).astype(jnp.bfloat16))
    get_proj = Gather(after(w_proj, *t).astype(jnp.bfloat16))
    get_up = Gather(after(w_up, *t).astype(jnp.bfloat16))
    t = (get_down.sent, get_proj.sent, get_up.sent)
    t = slot(t, [small, get_qkv[0]], [get_qkv[0], get_down, get_qkv[1]])
    t = slot(t, [get_qkv[0]])
    small = small.whole.astype(jnp.float32)
    g = small[: gains.shape[0]]
    embed = small[gains.shape[0] :]
    onehot = (group_ids[:, None] == jnp.arange(table.shape[0])[None, :]).astype(jnp.float32)
    added = jnp.sum(onehot[:, :, None] * embed[None], axis=1)[:, None, :]
    live = (jnp.arange(slots) < counts[0]).astype(jnp.int32)

    qkv = []
    a1, group = project_in(after(tokens, *t), added, g[0:1], get_qkv[0].parts())
    qkv.append(group)
    t = slot((group,), [get_down], [get_down, get_proj])
    attended = attn_fwd(after(group, *t), 0, half, 0, width)
    t = slot((attended[0],), [get_qkv[1], get_proj], [get_qkv[1], get_proj, get_up])
    attended = attn_fwd(after(group, *t), half, group_pairs - half, 0, width, attended)
    t = slot((attended[0],), [get_qkv[1], get_proj])
    _, group = project_in(after(tokens, *t), added, g[0:1], get_qkv[1].parts())
    qkv.append(group)
    attended = attn_fwd(group, 0, half, group_pairs, width, attended)
    t = slot((attended[0],), [get_up], [get_up])
    attended = attn_fwd(after(group, *t), half, group_pairs - half, group_pairs, width, attended)
    mixture, log_totals = attended
    t = slot((mixture,), [get_up])
    p_qkv = [w.parts() for w in get_qkv]
    p_proj, p_up, p_down = get_proj.parts(), get_up.parts(), get_down.parts()
    a3, f, slope, dm, z, h1, output, sums_out = up_and_down(
        live, after(mixture, *t), tokens, cotangent, added, g, p_proj, p_up, p_down
    )

    down = GradSum(flat(f), flat(dm), spread=True)
    t = down.part((dm,))
    t = slot(t, [], [down])
    t = slot(t, [down])
    t = slot(down.part(t), [], [down])
    du = back_to_hidden(after(dm, *t), slope, p_down)
    up = GradSum(flat(a3), flat(du), spread=True)
    t = up.part((du,))
    t = slot(t, [down], [down, up])
    t = slot(t, [up])
    t = slot(up.part(t), [], [up])
    dz, do, dh1, sums_mid = back_to_mixture(live, after(du, *t), h1, z, cotangent, g, p_proj, p_up)
    t = slot((dz,), [down], [down])
    proj = GradSum(flat(mixture), flat(dz))
    t = slot(proj.part(t), [], [proj])
    chunks = []

    def attend(i, t):
        group = i // 2
        chunks.append(attn_bwd(qkv[group], mixture, after(do, *t), log_totals, (i % 2) * half, half, group * group_pairs))
        return (chunks[-1],)

    t = attend(0, t)
    t = slot(t, [up, down, proj], [up, down])
    t = slot(proj.part(t), [], [proj])
    t = attend(1, t)
    t = slot(t, [up, down, proj], [up, down, proj])
    first = GradSum(flat(a1), [flat(d) for d in chunks])
    t = slot(first.part(t), [proj], [first, proj])
    t = attend(2, t)
    t = slot(t, [up, proj, first], [up, proj])
    t = slot(first.part(t), [proj], [first, proj])
    t = attend(3, t)
    t = slot(t, [up, first, proj], [up, first, proj])
    last = GradSum(flat(a1), [flat(d) for d in chunks[2:]])
    t = slot(last.part(t), [proj], [last, proj])
    t = slot(t, [last, first, proj], [first, proj])
    t = slot(last.part(t), [first], [last, first])

    backs = []
    for i in range(slots):
        backs.append(project_back(i, chunks, tokens, after(dh1, *t), added, g[0:1], p_qkv))
        t = (backs[-1][0],)
        if i == 0:
            t = slot(t, [last, first, proj], [last, first])
    grad_tokens, more = (jnp.concatenate(v, axis=0) for v in zip(*backs))
    grad_embed = jnp.sum(onehot[:, :, None] * more[:, None, 1, :], axis=0)
    grad_gains = jnp.concatenate([more[:, 0:1], sums_mid[:, 0:2], sums_out[:, 0:1]], axis=1).sum(axis=0)
    little = SmallSum(jnp.concatenate([grad_gains, grad_embed], axis=0))
    t = slot(t + (little.sent,) if paired() else t, [last, first], [last, first, little])
    grad_down = down.result(*t)
    t = slot((grad_down,), [last, first, little], [last, first, little])
    grad_proj = proj.result()
    t = slot((grad_proj,), [last, first, little], [last, first, little])
    while paired() and last.state != "done":
        moving = [e for e in (last, first) if e.state != "done"] + ([little] if little.bits else [])
        ending = [e for e in (last, first) if e.state != "done"] + ([little] if little.received is not None else [])
        t = slot(t, ending, [])
        moving = [e for e in (last, first) if e.state != "done"] + ([little] if little.bits else [])
        little.received = None
        if moving:
            t = slot(t, [], moving)
    if paired():
        grad_qkv = assemble([(e.kept, e.received) for e in (first, last)])
    else:
        part = first.total.shape[1] // 3
        grad_qkv = jnp.concatenate([e.total[:, i * part : (i + 1) * part] for i in range(3) for e in (first, last)], axis=1)
    small_sum = little.result()
    return (
        output,
        grad_tokens,
        grad_qkv,
        grad_proj,
        up.result(*t),
        grad_down,
        small_sum[: gains.shape[0]],
        small_sum[gains.shape[0] :],
    )


def solution(mesh):
    by_seq = P(("dp", "fsdp"), None, None)
    by_slot = P(("dp", "fsdp"))
    by_row = P("fsdp", None)
    by_col = P(None, "fsdp")
    return jax.shard_map(
        local,
        mesh=mesh,
        in_specs=(by_seq, by_seq, by_slot, by_slot) + (by_row,) * 4 + (by_col,) * 2,
        out_specs=(by_seq, by_seq) + (by_row,) * 4 + (by_col,) * 2,
        check_vma=False,
    )
```

```python
import math

import jax
import jax.numpy as jnp
from jax import lax
from jax.experimental import pallas as pl
from jax.experimental.pallas import tpu as pltpu
from jax.sharding import PartitionSpec as P

HEAD_DIM = 64
LANES = 128
EPSILON = 1e-05
NEG = -1e30
ATTN_ROWS = 256
VMEM_BYTES = 60 * 1024 * 1024


def dot(a, b, a_dim, b_dim):
    return lax.dot_general(a, b, (((a_dim,), (b_dim,)), ((), ())), preferred_element_type=jnp.float32)


def params(*semantics):
    return pltpu.CompilerParams(vmem_limit_bytes=VMEM_BYTES)


def row_block(length, most):
    return max(b for b in range(16, most + 1, 16) if length % b == 0)


def normed(rows):
    centered = rows - jnp.mean(rows, axis=-1, keepdims=True)
    inv_std = lax.rsqrt(jnp.mean(centered * centered, axis=-1, keepdims=True) + EPSILON)
    return centered * inv_std, inv_std


def halves(rows):
    middle = rows // 32 * 16
    return [slice(0, middle), slice(middle, rows)] if middle else [slice(0, rows)]


def norm_back(gradient, unit, inv_std, gain):
    grad_unit = gradient * gain
    first = jnp.mean(grad_unit, axis=-1, keepdims=True)
    second = jnp.mean(grad_unit * unit, axis=-1, keepdims=True)
    return inv_std * (grad_unit - first - unit * second)


def gelu_parts(u):
    cdf = 0.5 + 0.5 * lax.erf(u * math.sqrt(0.5))
    return u * cdf, cdf + u * jnp.exp(-0.5 * u * u) * (1.0 / math.sqrt(2.0 * math.pi))


def staged(jobs, one, two, three):
    n, firsts, seconds = len(jobs), {}, {}
    for i in range(n + 2):
        if i < n:
            firsts[i] = one(jobs[i])
        if i >= 2:
            three(jobs[i - 2], seconds.pop(i - 2))
        if 1 <= i <= n:
            seconds[i - 1] = two(jobs[i - 1], firsts.pop(i - 1))


def spans(length):
    return [(s, min(s + ATTN_ROWS, length)) for s in range(0, length, ATTN_ROWS)]


class Weights:
    def __init__(self, matrices):
        self.refs = [part[0] for parts, _ in matrices for part in parts]
        self.parts = [[part[1:] for part in parts] for parts, _ in matrices]
        self.shapes = [shape for _, shape in matrices]
        self.starts = jnp.stack([jnp.asarray(part[1], jnp.int32) for parts, _ in matrices for part in parts])
        self.in_specs = [pl.BlockSpec(memory_space=pl.ANY)] * len(self.refs)
        self.scratch = [pltpu.VMEM(shape, jnp.bfloat16) for shape in self.shapes]
        n_copies = sum(len(part[1]) if len(part) > 1 else 1 for parts in self.parts for part in parts)
        self.scratch.append(pltpu.SemaphoreType.DMA((n_copies,)))

    def copies(self, starts_ref, refs, scratch):
        lists, at, n = [], 0, 0
        for parts, whole in zip(self.parts, scratch[:-1]):
            mine = []
            for part in parts:
                rows = pl.ds(pl.multiple_of(starts_ref[at], 16), refs[at].shape[-2])
                pairs = [(refs[at], whole.at[..., rows, :])]
                if len(part) > 1:
                    pairs = [(refs[at].at[:, lo:hi], whole.at[i, rows, :]) for i, (lo, hi) in enumerate(part[1])]
                for source, target in pairs:
                    mine.append(pltpu.make_async_copy(source, target, scratch[-1].at[n]))
                    n += 1
                at += 1
            lists.append(mine)
        return lists


def run_all(copies, method):
    for copy in copies:
        getattr(copy, method)()


def norm_in(tokens, added, gain):
    slots, length, width = tokens.shape
    block = row_block(length, 544)

    def kernel(x_ref, e_ref, g_ref, a_ref):
        a_ref[0] = (normed(x_ref[0] + e_ref[0])[0] * g_ref[...]).astype(jnp.bfloat16)

    rows = pl.BlockSpec((1, block, width), lambda s, i: (s, i, 0))
    return pl.pallas_call(
        kernel,
        grid=(slots, length // block),
        in_specs=[rows, pl.BlockSpec((1, 1, width), lambda s, i: (s, 0, 0)), pl.BlockSpec((1, width), lambda s, i: (0, 0))],
        out_specs=rows,
        out_shape=jax.ShapeDtypeStruct(tokens.shape, jnp.bfloat16),
        compiler_params=params(),
        name="norm_in",
    )(tokens, added, gain)


def project_in(a1, weight):
    slots, length, width = a1.shape
    part = weight[1][2]
    block = row_block(length, 544)
    held = Weights([weight])
    n_held = len(held.refs)

    def kernel(starts_ref, a_ref, *rest):
        refs, out_ref, scratch = rest[:n_held], rest[n_held], rest[n_held + 1 :]

        @pl.when((pl.program_id(0) == 0) & (pl.program_id(1) == 0))
        def _():
            copies = held.copies(starts_ref, refs, scratch)[0]
            run_all(copies, "start")
            run_all(copies, "wait")

        for i in range(3):
            out_ref[i, 0] = dot(a_ref[0], scratch[0][i], 1, 0).astype(jnp.bfloat16)

    return pl.pallas_call(
        kernel,
        grid_spec=pltpu.PrefetchScalarGridSpec(
            num_scalar_prefetch=1,
            grid=(slots, length // block),
            in_specs=[pl.BlockSpec((1, block, width), lambda s, i, _: (s, i, 0))] + held.in_specs,
            out_specs=pl.BlockSpec((3, 1, block, part), lambda s, i, _: (0, s, i, 0)),
            scratch_shapes=held.scratch,
        ),
        out_shape=jax.ShapeDtypeStruct((3, slots, length, part), jnp.bfloat16),
        compiler_params=params(),
        name="project_in",
    )(held.starts, a1, *held.refs)


def causal(scores, keys_first):
    q = lax.broadcasted_iota(jnp.int32, scores.shape, 1 if keys_first else 0)
    k = lax.broadcasted_iota(jnp.int32, scores.shape, 0 if keys_first else 1)
    return q >= k


def attn_fwd_kernel(x_ref, o_ref, l_ref):
    length = x_ref.shape[2]
    first = lax.broadcasted_iota(jnp.int32, (1, LANES), 1) < HEAD_DIM
    jobs = [(lo, hi, h) for lo, hi in spans(length) for h in range(2)]
    outs = {}

    def scores(job):
        lo, hi, h = job
        q = x_ref[0, 0, lo:hi, :] * (1.0 / math.sqrt(HEAD_DIM))
        q = jnp.where(first if h == 0 else ~first, q, 0).astype(jnp.bfloat16)
        near = dot(q, x_ref[1, 0, lo:hi, :], 1, 1)
        near = jnp.where(causal(near, False), near, NEG)
        return near, dot(q, x_ref[1, 0, 0:lo, :], 1, 1) if lo else None

    def weights(job, both):
        near, far = both
        top = jnp.max(near, axis=1, keepdims=True)
        if far is not None:
            top = jnp.maximum(top, jnp.max(far, axis=1, keepdims=True))
        near = jnp.exp(near - top)
        total = jnp.sum(near, axis=1, keepdims=True)
        if far is not None:
            far = jnp.exp(far - top)
            total = total + jnp.sum(far, axis=1, keepdims=True)
            far = far.astype(jnp.bfloat16)
        return near.astype(jnp.bfloat16), far, top, total

    def mix(job, parts):
        lo, hi, h = job
        near, far, top, total = parts
        o = dot(near, x_ref[2, 0, lo:hi, :], 1, 0)
        if far is not None:
            o = o + dot(far, x_ref[2, 0, 0:lo, :], 1, 0)
        outs[h] = o / total
        log_total = jnp.broadcast_to(top + jnp.log(total), (hi - lo, LANES))
        l_ref[0, 0, h : h + 1, lo:hi] = jnp.transpose(log_total)[0:1, :]
        if h == 1:
            o_ref[0, lo:hi, :] = jnp.where(first, outs[0], outs[1]).astype(jnp.bfloat16)

    staged(jobs, scores, weights, mix)


def attn_fwd(qkv, start, count, first_pair, width, before=None):
    _, slots, length, _ = qkv.shape
    place = first_pair + start
    n_before = 0 if before is None else 2

    def kernel(x_ref, *rest):
        attn_fwd_kernel(x_ref, *rest[n_before:])

    return pl.pallas_call(
        kernel,
        grid=(slots, count),
        in_specs=[pl.BlockSpec((3, 1, length, LANES), lambda s, p: (0, s, 0, start + p))]
        + [pl.BlockSpec(memory_space=pl.ANY)] * n_before,
        out_specs=[
            pl.BlockSpec((1, length, LANES), lambda s, p: (s, 0, place + p)),
            pl.BlockSpec((1, 1, 2, length), lambda s, p: (s, place + p, 0, 0)),
        ],
        out_shape=[
            jax.ShapeDtypeStruct((slots, length, width), jnp.bfloat16),
            jax.ShapeDtypeStruct((slots, width // LANES, 2, length), jnp.float32),
        ],
        input_output_aliases={1 + i: i for i in range(n_before)},
        compiler_params=params(),
        name="attn_fwd",
    )(qkv, *(before or ()))


def attn_bwd_kernel(x_ref, o_ref, do_ref, l_ref, d_ref, dqt_ref):
    length = x_ref.shape[2]
    scale = 1.0 / math.sqrt(HEAD_DIM)
    first = lax.broadcasted_iota(jnp.int32, (1, LANES), 1) < HEAD_DIM
    q = x_ref[0, 0] * scale
    do = do_ref[0]
    prod = jnp.transpose(do.astype(jnp.float32) * o_ref[0].astype(jnp.float32))
    deltas = [jnp.sum(prod[:HEAD_DIM], axis=0, keepdims=True), jnp.sum(prod[HEAD_DIM:], axis=0, keepdims=True)]
    dqt_ref[...] = jnp.zeros_like(dqt_ref)
    jobs = []
    for lo, hi in spans(length):
        for h in range(2):
            jobs.append((lo, hi, h, lo, hi))
            if hi < length:
                jobs.append((lo, hi, h, hi, length))
    sums = {}

    def scores(job):
        lo, hi, h, a, b = job
        mine = lambda v: jnp.where(first if h == 0 else ~first, v, 0).astype(jnp.bfloat16)
        return dot(mine(x_ref[1, 0, lo:hi, :]), q[a:b], 1, 1), dot(mine(x_ref[2, 0, lo:hi, :]), do[a:b], 1, 1)

    def weights(job, both):
        lo, hi, h, a, b = job
        p = jnp.exp(both[0] - l_ref[0, 0, h : h + 1, a:b])
        if a == lo:
            p = jnp.where(causal(p, True), p, 0.0)
        return p.astype(jnp.bfloat16), (p * (both[1] - deltas[h][:, a:b])).astype(jnp.bfloat16)

    def collect(job, parts):
        lo, hi, h, a, b = job
        p, ds = parts
        dv, dk = dot(p, do[a:b], 1, 0), dot(ds, q[a:b], 1, 0)
        sums[h] = (dk, dv) if a == lo else (sums[h][0] + dk, sums[h][1] + dv)
        lanes = slice(h * HEAD_DIM, (h + 1) * HEAD_DIM)
        kt = jnp.transpose(x_ref[1, 0, lo:hi, :].astype(jnp.float32)).astype(jnp.bfloat16)
        dqt_ref[lanes, a:b] += dot(kt[lanes], ds, 1, 0)
        if h == 1 and b == length:
            for i in range(2):
                d_ref[1 + i, 0, lo:hi, :] = jnp.where(first, sums[0][i], sums[1][i]).astype(jnp.bfloat16)

    staged(jobs, scores, weights, collect)
    d_ref[0, 0] = (jnp.transpose(dqt_ref[...]) * scale).astype(jnp.bfloat16)


def attn_bwd(qkv, mixture, grad_mix, log_totals, start, count, first_pair):
    _, slots, length, _ = qkv.shape
    place = first_pair + start
    triple = pl.BlockSpec((3, 1, length, LANES), lambda s, p: (0, s, 0, start + p))
    single = pl.BlockSpec((1, length, LANES), lambda s, p: (s, 0, place + p))
    return pl.pallas_call(
        attn_bwd_kernel,
        grid=(slots, count),
        in_specs=[triple, single, single, pl.BlockSpec((1, 1, 2, length), lambda s, p: (s, place + p, 0, 0))],
        out_specs=pl.BlockSpec((3, 1, length, LANES), lambda s, p: (0, s, 0, p)),
        out_shape=jax.ShapeDtypeStruct((3, slots, length, count * LANES), jnp.bfloat16),
        scratch_shapes=[pltpu.VMEM((LANES, length), jnp.float32)],
        compiler_params=params(),
        name="attn_bwd",
    )(qkv, mixture, grad_mix, log_totals)


def token_specs(shape, block):
    slots, length, width = shape
    rows = pl.BlockSpec((1, block, width), lambda s, i, *_: (s, i, 0))
    per_slot = lambda n: pl.BlockSpec((1, n, width), lambda s, i, *_: (s, 0, 0))
    whole = lambda v: pl.BlockSpec(v.shape, lambda s, i, *_: (0,) * v.ndim)
    return rows, per_slot, whole


def up_and_down(live, mixture, tokens, cotangent, added, gains, w_proj, w_up, w_down):
    slots, length, width = tokens.shape
    hidden = w_up[1][1]
    block = row_block(length, 272)
    chunk = min(512, hidden)
    held = Weights([w_proj, w_up, w_down])
    n_held = len(held.refs)

    def kernel(starts_ref, live_ref, o_ref, x_ref, c_ref, e_ref, g_ref, *rest):
        refs = rest[:n_held]
        a_ref, f_ref, du_ref, dm_ref, z_ref, h_ref, out_ref, sum_ref = rest[n_held : n_held + 8]
        wp, wu, wd = rest[n_held + 8 : n_held + 11]
        slope_ref = rest[n_held + 12]

        @pl.when((pl.program_id(0) == 0) & (pl.program_id(1) == 0))
        def _():
            copies = held.copies(starts_ref, refs, rest[n_held + 8 : n_held + 12])
            for some in copies:
                run_all(some, "start")
            for some in copies:
                run_all(some, "wait")

        @pl.when(pl.program_id(1) == 0)
        def _():
            sum_ref[...] = jnp.zeros_like(sum_ref)

        alive = live_ref[pl.program_id(0)].astype(jnp.float32)
        parts = halves(block)
        cols = [slice(j, j + chunk) for j in range(0, hidden, chunk)]
        h1, a, m, dm = {}, {}, {}, {}
        zs = [dot(o_ref[0, r, :], wp[...], 1, 0) for r in parts]

        def enter(n):
            r = parts[n]
            z_ref[0, r, :] = zs[n]
            h1[n] = x_ref[0, r, :] + e_ref[0] + normed(zs[n])[0] * g_ref[1:2]
            h_ref[0, r, :] = h1[n]
            a[n] = (normed(h1[n])[0] * g_ref[2:3]).astype(jnp.bfloat16)
            a_ref[0, r, :] = a[n]

        def leave(n):
            r = parts[n]
            unit_m, inv_m = normed(m[n])
            out_ref[0, r, :] = alive * (h1[n] + unit_m * g_ref[3:4])
            dy = alive * c_ref[0, r, :]
            dm[n] = norm_back(dy, unit_m, inv_m, g_ref[3:4]).astype(jnp.bfloat16)
            dm_ref[0, r, :] = dm[n]
            sum_ref[0, 0:1] += jnp.sum(dy * unit_m, axis=0, keepdims=True)

        def raised(job):
            n, c = job
            u = dot(a[n], wu[:, c], 1, 0)
            if c is cols[1 % len(cols)] and n + 1 < len(parts):
                enter(n + 1)
            return u

        def activate(job, u):
            n, c = job
            f, slope = gelu_parts(u)
            f_ref[0, parts[n], c] = f.astype(jnp.bfloat16)
            slope_ref[parts[n], c] = slope.astype(jnp.bfloat16)
            return f.astype(jnp.bfloat16)

        def lower(job, f):
            n, c = job
            more = dot(f, wd[c, :], 1, 0)
            m[n] = m[n] + more if n in m else more
            if c is cols[-1]:
                leave(n)

        enter(0)
        staged([(n, c) for n in range(len(parts)) for c in cols], raised, activate, lower)
        dm = jnp.concatenate([dm[n] for n in range(len(parts))], axis=0)

        def lift(cols, df):
            du_ref[0, :, cols] = (df * slope_ref[:, cols].astype(jnp.float32)).astype(jnp.bfloat16)

        staged(cols, lambda c: dot(dm, wd[c, :], 1, 1), lift, lambda c, _: None)

    rows, per_slot, whole = token_specs(tokens.shape, block)
    wide = pl.BlockSpec((1, block, hidden), lambda s, i, *_: (s, i, 0))
    low = jax.ShapeDtypeStruct(tokens.shape, jnp.bfloat16)
    low_wide = jax.ShapeDtypeStruct((slots, length, hidden), jnp.bfloat16)
    full = jax.ShapeDtypeStruct(tokens.shape, jnp.float32)
    return pl.pallas_call(
        kernel,
        grid_spec=pltpu.PrefetchScalarGridSpec(
            num_scalar_prefetch=2,
            grid=(slots, length // block),
            in_specs=[rows, rows, rows, per_slot(1), whole(gains)] + held.in_specs,
            out_specs=[rows, wide, wide, rows, rows, rows, rows, per_slot(8)],
            scratch_shapes=held.scratch + [pltpu.VMEM((block, hidden), jnp.bfloat16)],
        ),
        out_shape=[low, low_wide, low_wide, low, full, full, full, jax.ShapeDtypeStruct((slots, 8, width), jnp.float32)],
        compiler_params=params(),
        name="up_and_down",
    )(held.starts, live, mixture, tokens, cotangent, added, gains, *held.refs)


def back_to_mixture(live, du, h1, z, cotangent, gains, w_proj, w_up):
    slots, length, width = h1.shape
    hidden = du.shape[-1]
    block = row_block(length, 272)
    held = Weights([w_up, w_proj])
    n_held = len(held.refs)

    def kernel(starts_ref, live_ref, du_ref, h_ref, z_ref, c_ref, g_ref, *rest):
        refs = rest[:n_held]
        dz_ref, do_ref, dh_ref, sum_ref = rest[n_held : n_held + 4]
        wu, wp = rest[n_held + 4 : n_held + 6]

        @pl.when((pl.program_id(0) == 0) & (pl.program_id(1) == 0))
        def _():
            copies = held.copies(starts_ref, refs, rest[n_held + 4 : n_held + 7])
            for some in copies:
                run_all(some, "start")
            for some in copies:
                run_all(some, "wait")

        @pl.when(pl.program_id(1) == 0)
        def _():
            sum_ref[...] = jnp.zeros_like(sum_ref)

        alive = live_ref[pl.program_id(0)].astype(jnp.float32)
        da = dot(du_ref[0], wu[...], 1, 1)
        unit_h, inv_h = normed(h_ref[0])
        unit_z, inv_z = normed(z_ref[0])
        dh1 = alive * c_ref[0] + norm_back(da, unit_h, inv_h, g_ref[2:3])
        dh_ref[0] = dh1
        dz = norm_back(dh1, unit_z, inv_z, g_ref[1:2]).astype(jnp.bfloat16)
        dz_ref[0] = dz
        do_ref[0] = dot(dz, wp[...], 1, 1).astype(jnp.bfloat16)
        sum_ref[0, 0:1] += jnp.sum(dh1 * unit_z, axis=0, keepdims=True)
        sum_ref[0, 1:2] += jnp.sum(da * unit_h, axis=0, keepdims=True)

    rows, per_slot, whole = token_specs(h1.shape, block)
    wide = pl.BlockSpec((1, block, hidden), lambda s, i, *_: (s, i, 0))
    low = jax.ShapeDtypeStruct(h1.shape, jnp.bfloat16)
    return pl.pallas_call(
        kernel,
        grid_spec=pltpu.PrefetchScalarGridSpec(
            num_scalar_prefetch=2,
            grid=(slots, length // block),
            in_specs=[wide, rows, rows, rows, whole(gains)] + held.in_specs,
            out_specs=[rows, rows, rows, per_slot(8)],
            scratch_shapes=held.scratch,
        ),
        out_shape=[
            low,
            low,
            jax.ShapeDtypeStruct(h1.shape, jnp.float32),
            jax.ShapeDtypeStruct((slots, 8, width), jnp.float32),
        ],
        compiler_params=params(),
        name="back_to_mixture",
    )(held.starts, live, du, h1, z, cotangent, gains, *held.refs)


def project_back(slot, part_of, groups, tokens, grad_middle, added, gain, weights, before=None):
    slots, length, width = tokens.shape
    block = row_block(length // part_of[1], 272)
    held = Weights(weights)
    per_weight = len(groups) // len(weights)
    n_held = len(held.refs)
    n_before = 0 if before is None else 2

    n_groups, part = len(groups), groups[0].shape[-1]
    steps = length // part_of[1] // block
    skip = part_of[0] * steps

    def kernel(starts_ref, *refs_in):
        d_refs, (x_ref, h_ref, e_ref, g_ref), rest = refs_in[:n_groups], refs_in[n_groups : n_groups + 4], refs_in[n_groups + 4 :]
        refs, rest = rest[:n_held], rest[n_held + n_before :]
        (out_ref, sum_ref), scratch = rest[:2], rest[2:]
        first = pl.program_id(0) == 0
        copies = sum(held.copies(starts_ref, refs, scratch), [])

        @pl.when(first)
        def _():
            run_all(copies, "start")

        unit, inv_std = normed(x_ref[0] + e_ref[0])

        @pl.when(first)
        def _():
            run_all(copies, "wait")

        da = None
        for w in range(len(weights)):
            mine = d_refs[w * per_weight : (w + 1) * per_weight]
            for i in range(3):
                more = dot(jnp.concatenate([ref[i, 0] for ref in mine], axis=1), scratch[w][i], 1, 1)
                da = more if da is None else da + more
        dh = h_ref[0] + norm_back(da, unit, inv_std, g_ref[...])
        out_ref[0] = dh

        @pl.when(pl.program_id(0) == 0)
        def _():
            sum_ref[...] = jnp.zeros_like(sum_ref)

        sum_ref[0, 0:1] += jnp.sum(da * unit, axis=0, keepdims=True)
        sum_ref[0, 1:2] += jnp.sum(dh, axis=0, keepdims=True)

    rows = pl.BlockSpec((1, block, width), lambda i, _: (slot, skip + i, 0))
    return pl.pallas_call(
        kernel,
        grid_spec=pltpu.PrefetchScalarGridSpec(
            num_scalar_prefetch=1,
            grid=(steps,),
            in_specs=[pl.BlockSpec((3, 1, block, part), lambda i, _: (0, slot, skip + i, 0))] * n_groups
            + [
                rows,
                rows,
                pl.BlockSpec((1, 1, width), lambda i, _: (slot, 0, 0)),
                pl.BlockSpec((1, width), lambda i, _: (0, 0)),
            ]
            + held.in_specs
            + [pl.BlockSpec(memory_space=pl.ANY)] * n_before,
            out_specs=[
                rows,
                pl.BlockSpec((1, 8, width), lambda i, _: (slot * part_of[1] + part_of[0], 0, 0)),
            ],
            scratch_shapes=held.scratch,
        ),
        out_shape=[
            jax.ShapeDtypeStruct(tokens.shape, jnp.float32),
            jax.ShapeDtypeStruct((slots * part_of[1], 8, width), jnp.float32),
        ],
        input_output_aliases={5 + n_groups + n_held + i: i for i in range(n_before)},
        compiler_params=params(),
        name="project_back",
    )(held.starts, *groups, tokens, grad_middle, added, gain, *held.refs, *(before or ()))


def columns_of(refs):
    if len(refs[0].shape) == 3:
        return jnp.concatenate([ref[0] for ref in refs], axis=1)
    return refs[0][...]


def grad_blocks(order, left, right, received=None):
    rows, depth = left.shape[0], left.shape[1] // 4
    tall = min(depth, 512)
    per_block = depth // tall
    stacked = isinstance(right, list)
    if stacked:
        count, slab = right[0].shape[0], sum(r.shape[-1] for r in right)
        right_specs = [pl.BlockSpec((1, rows, r.shape[-1]), lambda r, k, j, order: (j, 0, 0)) for r in right]
    else:
        slab = min(1024, right.shape[1])
        count = right.shape[1] // slab
        right_specs = [pl.BlockSpec((rows, slab), lambda r, k, j, order: (0, j))]
        right = [right]
    n_right = len(right)
    if depth <= 512:
        return narrow_grad_blocks(order, left, right, right_specs, (count, depth, slab), received)

    def kernel(order_ref, a_ref, *rest):
        right_block = columns_of(rest[:n_right])
        outs = rest[n_right:]
        total = dot(a_ref[...], right_block, 0, 0)
        if received is None:
            outs[0][0, 0] = total.astype(jnp.bfloat16)
            return
        total = (total + outs[0][0, 0].astype(jnp.float32)).astype(jnp.bfloat16)

        @pl.when(pl.program_id(0) == 0)
        def _():
            outs[1][0] = total

        @pl.when(pl.program_id(0) == 1)
        def _():
            outs[2][0] = total

    both = pl.BlockSpec((1, 1, tall, slab), lambda r, k, j, order: (r, j, k, 0))
    sent = pl.BlockSpec((1, tall, slab), lambda r, k, j, order: (jnp.where(r == 0, j, count - 1), jnp.where(r == 0, k, per_block - 1), 0))
    kept = pl.BlockSpec((1, tall, slab), lambda r, k, j, order: (jnp.where(r == 0, 0, j), jnp.where(r == 0, 0, k), 0))
    more = [] if received is None else [received]
    shape = (count, depth, slab)
    return pl.pallas_call(
        kernel,
        grid_spec=pltpu.PrefetchScalarGridSpec(
            num_scalar_prefetch=1,
            grid=(2, per_block, count),
            in_specs=[pl.BlockSpec((rows, tall), lambda r, k, j, order: (0, order[r] * per_block + k))]
            + right_specs
            + [both] * len(more),
            out_specs=[sent, kept] if more else both,
        ),
        out_shape=[jax.ShapeDtypeStruct(shape, jnp.bfloat16)] * 2 if more else jax.ShapeDtypeStruct((2,) + shape, jnp.bfloat16),
        compiler_params=params(),
        name="grad_blocks",
    )(order, left, *right, *more)


def narrow_grad_blocks(order, left, right, right_specs, shape, received):
    count, depth, slab = shape
    rows, n_right = left.shape[0], len(right)

    def kernel(order_ref, a0_ref, a1_ref, *rest):
        right_block = columns_of(rest[:n_right])
        outs = rest[n_right:]
        for r, a_ref in enumerate((a0_ref, a1_ref)):
            total = dot(a_ref[...], right_block, 0, 0)
            if received is None:
                outs[0][r, 0] = total.astype(jnp.bfloat16)
            else:
                outs[1 + r][0] = (total + outs[0][r, 0].astype(jnp.float32)).astype(jnp.bfloat16)

    by_step = lambda spec: pl.BlockSpec(spec.block_shape, lambda j, order: spec.index_map(0, 0, j, order))
    both = pl.BlockSpec((2, 1, depth, slab), lambda j, order: (0, j, 0, 0))
    one = pl.BlockSpec((1, depth, slab), lambda j, order: (j, 0, 0))
    left_spec = lambda r: pl.BlockSpec((rows, depth), lambda j, order: (0, order[r]), pipeline_mode=pl.Buffered(1))
    more = [] if received is None else [received]
    return pl.pallas_call(
        kernel,
        grid_spec=pltpu.PrefetchScalarGridSpec(
            num_scalar_prefetch=1,
            grid=(count,),
            in_specs=[left_spec(0), left_spec(1)] + [by_step(spec) for spec in right_specs] + [both] * len(more),
            out_specs=[one, one] if more else both,
        ),
        out_shape=[jax.ShapeDtypeStruct(shape, jnp.bfloat16)] * 2 if more else jax.ShapeDtypeStruct((2,) + shape, jnp.bfloat16),
        compiler_params=params(),
        name="grad_blocks",
    )(order, left, left, *right, *more)


def after(value, *earlier):
    return lax.optimization_barrier((value,) + earlier)[0]


def swap(value, axis, bit):
    size = lax.axis_size(axis)
    return lax.ppermute(value, axis, [(i, i ^ (1 << bit)) for i in range(size)])


def bit_of(axis, bit):
    return (lax.axis_index(axis) >> bit) & 1


def bits_of(axis):
    return range(lax.axis_size(axis).bit_length() - 1)


def pick(value, index):
    return lax.dynamic_index_in_dim(value, index, 0, keepdims=False)


def paired():
    return lax.axis_size("fsdp") == 2 and lax.axis_size("dp") % 2 == 0


def slot(before, ends=(), starts=()):
    before = tuple(before)
    if not paired():
        for e in ends:
            e.take()
        return before
    if ends:
        arrived = lax.optimization_barrier(tuple(e.received for e in ends) + before)
        for e, value in zip(ends, arrived):
            e.received = value
            e.take()
        before = arrived[len(ends) :]
    if starts:
        leaving = lax.optimization_barrier(tuple(e.sent for e in starts) + before)
        for e, value in zip(starts, leaving):
            e.send(value)
        before = leaving
    return before


class Gather:
    def __init__(self, low, ranges=None):
        self.low, self.ranges = low, ranges
        self.size, wide = low.shape
        whole = self.size * lax.axis_size("fsdp")
        self.shape = (whole, wide) if ranges is None else (len(ranges), whole, ranges[0][1] - ranges[0][0])
        self.crossed = None
        if paired():
            half = self.size // 2
            mine = lambda lo, hi: lax.dynamic_slice(low, (bit_of("dp", 0) * half, lo), (half, hi - lo))
            self.sent = mine(0, wide) if ranges is None else jnp.stack([mine(lo, hi) for lo, hi in ranges])
        else:
            self.sent = low

    def send(self, value):
        self.received = swap(value, "fsdp" if self.crossed is None else "dp", 0)

    def take(self):
        if not paired():
            return
        if self.crossed is None:
            self.crossed = self.sent = self.received
        else:
            self.beside = self.received

    def parts(self):
        ranges = () if self.ranges is None else (self.ranges,)
        if not paired():
            return [(lax.all_gather(self.low, "fsdp", axis=0, tiled=True), 0) + ranges], self.shape
        size, c, x = self.size, bit_of("dp", 0), lax.axis_index("fsdp")
        base = (1 - x) * size
        own = (self.low, x * size) + ranges
        return [own, (self.crossed, base + c * (size // 2)), (self.beside, base + (1 - c) * (size // 2))], self.shape


class WideGather:
    def __init__(self, low):
        self.low = low
        self.shape = (low.shape[0] * lax.axis_size("fsdp"), low.shape[1])
        self.crossed = None
        self.sent = low
        if paired():
            n_dp = lax.axis_size("dp")
            self.sent = pick(low.reshape(n_dp, low.shape[0] // n_dp, low.shape[1]), lax.axis_index("dp"))

    def send(self, value):
        if self.crossed is None:
            self.received = swap(value, "fsdp", 0)
        else:
            self.other = lax.all_gather(value, "dp", axis=0, tiled=True)

    def take(self):
        if paired():
            self.crossed = self.sent = self.received

    def parts(self):
        if not paired():
            return [(lax.all_gather(self.low, "fsdp", axis=0, tiled=True), 0)], self.shape
        size, x = self.low.shape[0], lax.axis_index("fsdp")
        return [(self.low, x * size), (self.other, (1 - x) * size)], self.shape


class Columns:
    def __init__(self, low):
        self.low = self.sent = low

    def send(self, value):
        self.received = swap(value, "fsdp", 0)

    def take(self):
        if not paired():
            self.whole = lax.all_gather(self.low, "fsdp", axis=1, tiled=True)
            return
        first = lax.axis_index("fsdp") == 0
        self.whole = jnp.concatenate(
            [jnp.where(first, self.low, self.received), jnp.where(first, self.received, self.low)], axis=1
        )


class SmallSum:
    def __init__(self, value):
        self.value, self.bits = value, None
        if paired():
            halves = value.reshape(value.shape[0], 2, -1)
            x = lax.axis_index("fsdp")
            self.value = lax.dynamic_index_in_dim(halves, x, 1, keepdims=False)
            self.sent = lax.dynamic_index_in_dim(halves, 1 - x, 1, keepdims=False)

    def send(self, value):
        if self.bits is None:
            self.bits = list(bits_of("dp"))
            self.received = swap(value, "fsdp", 0)
        else:
            self.received = swap(value, "dp", self.bits.pop(0))

    def take(self):
        if paired():
            self.value = self.sent = self.value + self.received

    def result(self):
        if paired():
            return self.value
        return lax.psum(lax.psum_scatter(self.value, "fsdp", scatter_dimension=1, tiled=True), "dp")


def assemble(pieces):
    count, rows, wide = pieces[0][0].shape
    n_pieces = len(pieces)

    def kernel(c_ref, *refs):
        out_ref = refs[-1]
        for p in range(n_pieces):

            @pl.when(pl.program_id(1) == p)
            def _():
                for i, ref in enumerate(refs[2 * p : 2 * p + 2]):
                    half = c_ref[0] if i == 0 else 1 - c_ref[0]
                    out_ref[pl.ds(pl.multiple_of(half * rows, rows), rows), :] = ref[0].astype(jnp.float32)

    return pl.pallas_call(
        kernel,
        grid_spec=pltpu.PrefetchScalarGridSpec(
            num_scalar_prefetch=1,
            grid=(count, n_pieces),
            in_specs=[pl.BlockSpec((1, rows, wide), lambda i, p, c: (i, 0, 0))] * (2 * n_pieces),
            out_specs=pl.BlockSpec((2 * rows, wide), lambda i, p, c: (0, i * n_pieces + p)),
        ),
        out_shape=jax.ShapeDtypeStruct((2 * rows, count * n_pieces * wide), jnp.float32),
        compiler_params=params(),
        name="assemble",
    )(bit_of("dp", 0).astype(jnp.int32).reshape(1), *[v for piece in pieces for v in piece])


def in_rows(whole):
    n, count, rows, wide = whole.shape
    n_bits = n.bit_length() - 1
    step = min(wide, 512)

    def place(i):
        return sum(((i >> (n_bits - 1 - b)) & 1) << b for b in range(n_bits))

    def kernel(in_ref, out_ref):
        for i in range(n):
            out_ref[place(i) * rows : (place(i) + 1) * rows, :] = in_ref[i, 0].astype(jnp.float32)

    return pl.pallas_call(
        kernel,
        grid=(count, wide // step),
        in_specs=[pl.BlockSpec((n, 1, rows, step), lambda s, j: (0, s, 0, j))],
        out_specs=pl.BlockSpec((n * rows, step), lambda s, j: (0, s * (wide // step) + j)),
        out_shape=jax.ShapeDtypeStruct((n * rows, count * wide), jnp.float32),
        compiler_params=params(),
        name="in_rows",
    )(whole)


class GradSum:
    def __init__(self, left, right, spread=False):
        self.left, self.right, self.spread = left, right, spread
        self.state = "send"
        if paired():
            self.bits = list(bits_of("dp"))[1:]

    def part(self, before):
        if not paired():
            if self.state == "send":
                right = self.right
                if isinstance(right, list):
                    right = jnp.concatenate([r[i] for i in range(3) for r in right], axis=1)
                low = dot(self.left, right, 0, 0).astype(jnp.bfloat16)
                piece = lax.psum_scatter(low, ("fsdp", "dp"), scatter_dimension=0, tiled=True)
                self.total = lax.all_gather(piece, "dp", axis=0, tiled=True).astype(jnp.float32)
                self.state = "keep"
            return before
        c, x = bit_of("dp", 0), lax.axis_index("fsdp")
        left = after(self.left, *before)
        if self.state == "send":
            order = jnp.stack([(1 - x) * 2 + 1 - c, x * 2 + 1 - c]).astype(jnp.int32)
            self.sent = grad_blocks(order, left, self.right)
        else:
            order = jnp.stack([(1 - x) * 2 + c, x * 2 + c]).astype(jnp.int32)
            self.sent, self.kept = grad_blocks(order, left, self.right, self.received)
        return (self.sent,)

    def send(self, value):
        if self.state == "send":
            self.received = swap(value, "dp", 0)
        elif self.state == "keep":
            self.received = swap(value, "fsdp", 0)
        elif self.state == "halve":
            self.received = swap(value, "dp", self.bit)
        elif self.spread:
            self.whole = lax.all_gather(value, "dp", axis=0, tiled=False)
        else:
            self.received = swap(value, "dp", self.bit)

    def take(self):
        if not paired():
            return
        if self.state == "send":
            self.state = "keep"
        elif self.state in ("keep", "halve"):
            if self.bits:
                self.state, self.bit = "halve", self.bits.pop(0)
                b = bit_of("dp", self.bit)
                slabs, rows, wide = self.kept.shape
                kept, received = (v.reshape(slabs, 2, rows // 2, wide) for v in (self.kept, self.received))
                part = lambda v, i: lax.dynamic_index_in_dim(v, i, 1, keepdims=False).astype(jnp.float32)
                self.sent = (part(kept, 1 - b) + part(received, 1 - b)).astype(jnp.bfloat16)
                self.kept = (part(kept, b) + part(received, b)).astype(jnp.bfloat16)
            else:
                self.kept = self.sent = (self.kept.astype(jnp.float32) + self.received.astype(jnp.float32)).astype(jnp.bfloat16)
                self.state, self.bits = "join", list(bits_of("dp"))
                self.bit = self.bits.pop()
        elif self.bits:
            self.kept = self.sent = in_order(self.kept, self.received, bit_of("dp", self.bit))
            self.bit = self.bits.pop()
        else:
            self.state = "done"

    def result(self, *earlier):
        if not paired():
            return self.total
        if self.spread:
            return in_rows(after(self.whole, *earlier))
        return assemble([(after(self.kept, *earlier), self.received)])


def in_order(mine, other, bit):
    return jnp.where(bit == 0, jnp.concatenate([mine, other], axis=1), jnp.concatenate([other, mine], axis=1))


def local(tokens, cotangent, group_ids, counts, w_qkv, w_proj, w_up, w_down, gains, table):
    slots, length, width = tokens.shape
    rows = slots * length
    flat = lambda v: v.reshape(v.shape[:-3] + (rows, v.shape[-1]))
    pairs = width // LANES
    n_groups = 2
    group_pairs = pairs // n_groups
    half = group_pairs // 2
    part = width // n_groups
    small = Columns(jnp.concatenate([gains, table], axis=0).astype(jnp.bfloat16))
    low_qkv = w_qkv.astype(jnp.bfloat16)
    get_qkv = [
        Gather(low_qkv, [(i * width + j * part, i * width + (j + 1) * part) for i in range(3)]) for j in range(n_groups)
    ]
    t = slot((), starts=[small, get_qkv[0]])
    get_down = WideGather(after(w_down, *t).astype(jnp.bfloat16))
    get_proj = Gather(after(w_proj, *t).astype(jnp.bfloat16))
    get_up = Gather(after(w_up, *t).astype(jnp.bfloat16))
    t = (get_down.sent, get_proj.sent, get_up.sent)
    t = slot(t, [small])
    small = small.whole.astype(jnp.float32)
    g = small[: gains.shape[0]]
    embed = small[gains.shape[0] :]
    onehot = (group_ids[:, None] == jnp.arange(table.shape[0])[None, :]).astype(jnp.float32)
    added = jnp.sum(onehot[:, :, None] * embed[None], axis=1)[:, None, :]
    live = (jnp.arange(slots) < counts[0]).astype(jnp.int32)
    a1 = norm_in(after(tokens, *t), added, g[0:1])
    t = slot((a1,), [get_qkv[0]], [get_qkv[0], get_qkv[1]])
    t = slot(t, [get_qkv[0]])

    qkv = []
    group = project_in(after(a1, *t), get_qkv[0].parts())
    qkv.append(group)
    t = slot((group,), [get_qkv[1]], [get_qkv[1], get_down, get_up])
    attended = attn_fwd(after(group, *t), 0, half, 0, width)
    t = slot((attended[0],), [get_qkv[1], get_down], [get_down, get_proj])
    attended = attn_fwd(after(group, *t), half, group_pairs - half, 0, width, attended)
    t = (attended[0],)
    group = project_in(after(a1, *t), get_qkv[1].parts())
    qkv.append(group)
    mixture, log_totals = attn_fwd(group, 0, group_pairs, group_pairs, width, attended)
    t = slot((mixture,), [get_up, get_proj], [get_up, get_proj])
    t = slot(t, [get_up, get_proj])
    p_qkv = [w.parts() for w in get_qkv]
    p_proj, p_up, p_down = get_proj.parts(), get_up.parts(), get_down.parts()
    a3, f, du, dm, z, h1, output, sums_out = up_and_down(
        live, after(mixture, *t), tokens, cotangent, added, g, p_proj, p_up, p_down
    )

    down = GradSum(flat(f), flat(dm), spread=True)
    up = GradSum(flat(a3), flat(du), spread=True)
    t = slot(down.part((dm,)), [], [down])
    t = slot(up.part(t), [down], [up])
    t = slot(down.part(t), [up], [down])
    t = up.part(t)
    dz, do, dh1, sums_mid = back_to_mixture(live, after(du, *t), h1, z, cotangent, g, p_proj, p_up)
    t = slot((dz,), [down], [down, up])
    proj = GradSum(flat(mixture), flat(dz))
    t = slot(proj.part(t), [], [proj])
    chunks = []

    def attend(i, t):
        group = i // 2
        chunks.append(attn_bwd(qkv[group], mixture, after(do, *t), log_totals, (i % 2) * half, half, group * group_pairs))
        return (chunks[-1],)

    t = attend(0, t)
    t = slot(t, [down, proj], [down])
    t = slot(proj.part(t), [], [proj])
    t = attend(1, t)
    t = slot(t, [up, down, proj], [up, down, proj])
    first = GradSum(flat(a1), [flat(d) for d in chunks])
    t = slot(first.part(t), [proj], [first, proj])
    t = attend(2, t)
    t = slot(t, [up, down, first, proj], [up, down, proj])
    t = slot(first.part(t), [proj], [first, proj])
    t = attend(3, t)
    t = slot(t, [up, first, proj], [up, first, proj])
    last = GradSum(flat(a1), [flat(d) for d in chunks[2:]])
    t = slot(last.part(t), [proj], [last, proj])
    grad_down = down.result(*t)
    t = slot((grad_down,), [last])
    t = slot(last.part(t), [up, first, proj], [up, last, first, proj])
    back = project_back(0, (0, 1), chunks, tokens, after(dh1, *t), added, g[0:1], p_qkv)
    t = slot((back[0],), [last, first, proj], [last, first])
    back = project_back(1, (0, 1), chunks, tokens, after(dh1, *t), added, g[0:1], p_qkv, back)
    grad_tokens, more = back
    grad_embed = jnp.sum(onehot[:, :, None] * more[:, None, 1, :], axis=0)
    grad_gains = jnp.concatenate([more[:, 0:1], sums_mid[:, 0:2], sums_out[:, 0:1]], axis=1).sum(axis=0)
    little = SmallSum(jnp.concatenate([grad_gains, grad_embed], axis=0))
    t = slot((more, little.sent) if paired() else (more,), [last, first], [last, first, little])
    grad_proj = proj.result(*t)
    t = slot((grad_proj,), [last, first, little], [last, first, little])
    grad_up = up.result(*t)
    t = (grad_up,)
    waiting = [last, first, little]
    while paired() and last.state != "done":
        t = slot(t, waiting)
        waiting = [e for e in (last, first) if e.state != "done"] + ([little] if little.bits else [])
        if waiting:
            t = slot(t, [], waiting)
    if paired():
        grad_qkv = assemble([(e.kept, e.received) for e in (first, last)])
    else:
        part = first.total.shape[1] // 3
        grad_qkv = jnp.concatenate([e.total[:, i * part : (i + 1) * part] for i in range(3) for e in (first, last)], axis=1)
    small_sum = little.result()
    return (
        output,
        grad_tokens,
        grad_qkv,
        grad_proj,
        grad_up,
        grad_down,
        small_sum[: gains.shape[0]],
        small_sum[gains.shape[0] :],
    )


def solution(mesh):
    by_seq = P(("dp", "fsdp"), None, None)
    by_slot = P(("dp", "fsdp"))
    by_row = P("fsdp", None)
    by_col = P(None, "fsdp")
    return jax.shard_map(
        local,
        mesh=mesh,
        in_specs=(by_seq, by_seq, by_slot, by_slot) + (by_row,) * 4 + (by_col,) * 2,
        out_specs=(by_seq, by_seq) + (by_row,) * 4 + (by_col,) * 2,
        check_vma=False,
    )
```

```python
import math

import jax
import jax.numpy as jnp
from jax import lax
from jax.experimental import pallas as pl
from jax.experimental.pallas import tpu as pltpu
from jax.sharding import PartitionSpec as P

HEAD_DIM = 64
LANES = 128
EPSILON = 1e-05
NEG = -1e30
ATTN_ROWS = 256
VMEM_BYTES = 60 * 1024 * 1024


def dot(a, b, a_dim, b_dim):
    return lax.dot_general(a, b, (((a_dim,), (b_dim,)), ((), ())), preferred_element_type=jnp.float32)


def params(*semantics):
    return pltpu.CompilerParams(vmem_limit_bytes=VMEM_BYTES)


def row_block(length, most):
    return max(b for b in range(16, most + 1, 16) if length % b == 0)


def normed(rows):
    centered = rows - jnp.mean(rows, axis=-1, keepdims=True)
    inv_std = lax.rsqrt(jnp.mean(centered * centered, axis=-1, keepdims=True) + EPSILON)
    return centered * inv_std, inv_std


def halves(rows):
    middle = rows // 32 * 16
    return [slice(0, middle), slice(middle, rows)] if middle else [slice(0, rows)]


def norm_back(gradient, unit, inv_std, gain):
    grad_unit = gradient * gain
    first = jnp.mean(grad_unit, axis=-1, keepdims=True)
    second = jnp.mean(grad_unit * unit, axis=-1, keepdims=True)
    return inv_std * (grad_unit - first - unit * second)


def gelu_parts(u):
    cdf = 0.5 + 0.5 * lax.erf(u * math.sqrt(0.5))
    return u * cdf, cdf + u * jnp.exp(-0.5 * u * u) * (1.0 / math.sqrt(2.0 * math.pi))


def staged(jobs, one, two, three):
    n, firsts, seconds = len(jobs), {}, {}
    for i in range(n + 2):
        if i < n:
            firsts[i] = one(jobs[i])
        if i >= 2:
            three(jobs[i - 2], seconds.pop(i - 2))
        if 1 <= i <= n:
            seconds[i - 1] = two(jobs[i - 1], firsts.pop(i - 1))


def spans(length):
    return [(s, min(s + ATTN_ROWS, length)) for s in range(0, length, ATTN_ROWS)]


class Weights:
    def __init__(self, matrices):
        self.refs = [part[0] for parts, _ in matrices for part in parts]
        self.parts = [[part[1:] for part in parts] for parts, _ in matrices]
        self.shapes = [shape for _, shape in matrices]
        self.starts = jnp.stack([jnp.asarray(part[1], jnp.int32) for parts, _ in matrices for part in parts])
        self.in_specs = [pl.BlockSpec(memory_space=pl.ANY)] * len(self.refs)
        self.scratch = [pltpu.VMEM(shape, jnp.bfloat16) for shape in self.shapes]
        n_copies = sum(len(part[1]) if len(part) > 1 else 1 for parts in self.parts for part in parts)
        self.scratch.append(pltpu.SemaphoreType.DMA((n_copies,)))

    def copies(self, starts_ref, refs, scratch):
        lists, at, n = [], 0, 0
        for parts, whole in zip(self.parts, scratch[:-1]):
            mine = []
            for part in parts:
                rows = pl.ds(pl.multiple_of(starts_ref[at], 16), refs[at].shape[-2])
                pairs = [(refs[at], whole.at[..., rows, :])]
                if len(part) > 1:
                    pairs = [(refs[at].at[:, lo:hi], whole.at[i, rows, :]) for i, (lo, hi) in enumerate(part[1])]
                for source, target in pairs:
                    mine.append(pltpu.make_async_copy(source, target, scratch[-1].at[n]))
                    n += 1
                at += 1
            lists.append(mine)
        return lists


def run_all(copies, method):
    for copy in copies:
        getattr(copy, method)()


def norm_in(tokens, added, gain):
    slots, length, width = tokens.shape
    block = row_block(length, 544)

    def kernel(x_ref, e_ref, g_ref, a_ref):
        a_ref[0] = (normed(x_ref[0] + e_ref[0])[0] * g_ref[...]).astype(jnp.bfloat16)

    rows = pl.BlockSpec((1, block, width), lambda s, i: (s, i, 0))
    return pl.pallas_call(
        kernel,
        grid=(slots, length // block),
        in_specs=[rows, pl.BlockSpec((1, 1, width), lambda s, i: (s, 0, 0)), pl.BlockSpec((1, width), lambda s, i: (0, 0))],
        out_specs=rows,
        out_shape=jax.ShapeDtypeStruct(tokens.shape, jnp.bfloat16),
        compiler_params=params(),
        name="norm_in",
    )(tokens, added, gain)


def project_in(a1, weight):
    slots, length, width = a1.shape
    part = weight[1][2]
    block = row_block(length, 544)
    held = Weights([weight])
    n_held = len(held.refs)

    def kernel(starts_ref, a_ref, *rest):
        refs, out_ref, scratch = rest[:n_held], rest[n_held], rest[n_held + 1 :]

        @pl.when((pl.program_id(0) == 0) & (pl.program_id(1) == 0))
        def _():
            copies = held.copies(starts_ref, refs, scratch)[0]
            run_all(copies, "start")
            run_all(copies, "wait")

        for i in range(3):
            out_ref[i, 0] = dot(a_ref[0], scratch[0][i], 1, 0).astype(jnp.bfloat16)

    return pl.pallas_call(
        kernel,
        grid_spec=pltpu.PrefetchScalarGridSpec(
            num_scalar_prefetch=1,
            grid=(slots, length // block),
            in_specs=[pl.BlockSpec((1, block, width), lambda s, i, _: (s, i, 0))] + held.in_specs,
            out_specs=pl.BlockSpec((3, 1, block, part), lambda s, i, _: (0, s, i, 0)),
            scratch_shapes=held.scratch,
        ),
        out_shape=jax.ShapeDtypeStruct((3, slots, length, part), jnp.bfloat16),
        compiler_params=params(),
        name="project_in",
    )(held.starts, a1, *held.refs)


def causal(scores, keys_first):
    q = lax.broadcasted_iota(jnp.int32, scores.shape, 1 if keys_first else 0)
    k = lax.broadcasted_iota(jnp.int32, scores.shape, 0 if keys_first else 1)
    return q >= k


def attn_fwd_kernel(x_ref, o_ref, l_ref):
    length = x_ref.shape[2]
    first = lax.broadcasted_iota(jnp.int32, (1, LANES), 1) < HEAD_DIM
    jobs = [(lo, hi, h) for lo, hi in spans(length) for h in range(2)]
    outs = {}

    def scores(job):
        lo, hi, h = job
        q = x_ref[0, 0, lo:hi, :] * (1.0 / math.sqrt(HEAD_DIM))
        q = jnp.where(first if h == 0 else ~first, q, 0).astype(jnp.bfloat16)
        near = dot(q, x_ref[1, 0, lo:hi, :], 1, 1)
        near = jnp.where(causal(near, False), near, NEG)
        return near, dot(q, x_ref[1, 0, 0:lo, :], 1, 1) if lo else None

    def weights(job, both):
        near, far = both
        top = jnp.max(near, axis=1, keepdims=True)
        if far is not None:
            top = jnp.maximum(top, jnp.max(far, axis=1, keepdims=True))
        near = jnp.exp(near - top)
        if far is not None:
            far = jnp.exp(far - top).astype(jnp.bfloat16)
        return near.astype(jnp.bfloat16), far, top

    def with_ones(a, b):
        v = x_ref[2, 0, a:b, :]
        return jnp.concatenate([v, jnp.ones_like(v)], axis=1)

    def mix(job, parts):
        lo, hi, h = job
        near, far, top = parts
        o = dot(near, with_ones(lo, hi), 1, 0)
        if far is not None:
            o = o + dot(far, with_ones(0, lo), 1, 0)
        o, total = o[:, :LANES], o[:, LANES:]
        outs[h] = o / total
        log_total = top + jnp.log(total)
        l_ref[0, 0, h : h + 1, lo:hi] = jnp.transpose(log_total)[0:1, :]
        if h == 1:
            o_ref[0, lo:hi, :] = jnp.where(first, outs[0], outs[1]).astype(jnp.bfloat16)

    staged(jobs, scores, weights, mix)


def attn_fwd(qkv, start, count, first_pair, width, before=None):
    _, slots, length, _ = qkv.shape
    place = first_pair + start
    n_before = 0 if before is None else 2

    def kernel(x_ref, *rest):
        attn_fwd_kernel(x_ref, *rest[n_before:])

    return pl.pallas_call(
        kernel,
        grid=(slots, count),
        in_specs=[pl.BlockSpec((3, 1, length, LANES), lambda s, p: (0, s, 0, start + p))]
        + [pl.BlockSpec(memory_space=pl.ANY)] * n_before,
        out_specs=[
            pl.BlockSpec((1, length, LANES), lambda s, p: (s, 0, place + p)),
            pl.BlockSpec((1, 1, 2, length), lambda s, p: (s, place + p, 0, 0)),
        ],
        out_shape=[
            jax.ShapeDtypeStruct((slots, length, width), jnp.bfloat16),
            jax.ShapeDtypeStruct((slots, width // LANES, 2, length), jnp.float32),
        ],
        input_output_aliases={1 + i: i for i in range(n_before)},
        compiler_params=params(),
        name="attn_fwd",
    )(qkv, *(before or ()))


def attn_bwd_kernel(x_ref, o_ref, do_ref, l_ref, d_ref, dqt_ref):
    length = x_ref.shape[2]
    scale = 1.0 / math.sqrt(HEAD_DIM)
    first = lax.broadcasted_iota(jnp.int32, (1, LANES), 1) < HEAD_DIM
    q = x_ref[0, 0] * scale
    do = do_ref[0]
    prod = jnp.transpose(do.astype(jnp.float32) * o_ref[0].astype(jnp.float32))
    deltas = [jnp.sum(prod[:HEAD_DIM], axis=0, keepdims=True), jnp.sum(prod[HEAD_DIM:], axis=0, keepdims=True)]
    dqt_ref[...] = jnp.zeros_like(dqt_ref)
    jobs = []
    for lo, hi in spans(length):
        for h in range(2):
            jobs.append((lo, hi, h, lo, hi))
            if hi < length:
                jobs.append((lo, hi, h, hi, length))
    sums = {}

    def scores(job):
        lo, hi, h, a, b = job
        mine = lambda v: jnp.where(first if h == 0 else ~first, v, 0).astype(jnp.bfloat16)
        return dot(mine(x_ref[1, 0, lo:hi, :]), q[a:b], 1, 1), dot(mine(x_ref[2, 0, lo:hi, :]), do[a:b], 1, 1)

    def weights(job, both):
        lo, hi, h, a, b = job
        p = jnp.exp(both[0] - l_ref[0, 0, h : h + 1, a:b])
        if a == lo:
            p = jnp.where(causal(p, True), p, 0.0)
        return p.astype(jnp.bfloat16), (p * (both[1] - deltas[h][:, a:b])).astype(jnp.bfloat16)

    def collect(job, parts):
        lo, hi, h, a, b = job
        p, ds = parts
        dv, dk = dot(p, do[a:b], 1, 0), dot(ds, q[a:b], 1, 0)
        sums[h] = (dk, dv) if a == lo else (sums[h][0] + dk, sums[h][1] + dv)
        lanes = slice(h * HEAD_DIM, (h + 1) * HEAD_DIM)
        kt = jnp.transpose(x_ref[1, 0, lo:hi, :].astype(jnp.float32)).astype(jnp.bfloat16)
        dqt_ref[lanes, a:b] += dot(kt[lanes], ds, 1, 0)
        if h == 1 and b == length:
            for i in range(2):
                d_ref[1 + i, 0, lo:hi, :] = jnp.where(first, sums[0][i], sums[1][i]).astype(jnp.bfloat16)

    staged(jobs, scores, weights, collect)
    d_ref[0, 0] = (jnp.transpose(dqt_ref[...]) * scale).astype(jnp.bfloat16)


def attn_bwd(qkv, mixture, grad_mix, log_totals, start, count, first_pair):
    _, slots, length, _ = qkv.shape
    place = first_pair + start
    triple = pl.BlockSpec((3, 1, length, LANES), lambda s, p: (0, s, 0, start + p))
    single = pl.BlockSpec((1, length, LANES), lambda s, p: (s, 0, place + p))
    return pl.pallas_call(
        attn_bwd_kernel,
        grid=(slots, count),
        in_specs=[triple, single, single, pl.BlockSpec((1, 1, 2, length), lambda s, p: (s, place + p, 0, 0))],
        out_specs=pl.BlockSpec((3, 1, length, LANES), lambda s, p: (0, s, 0, p)),
        out_shape=jax.ShapeDtypeStruct((3, slots, length, count * LANES), jnp.bfloat16),
        scratch_shapes=[pltpu.VMEM((LANES, length), jnp.float32)],
        compiler_params=params(),
        name="attn_bwd",
    )(qkv, mixture, grad_mix, log_totals)


def token_specs(shape, block):
    slots, length, width = shape
    rows = pl.BlockSpec((1, block, width), lambda s, i, *_: (s, i, 0))
    per_slot = lambda n: pl.BlockSpec((1, n, width), lambda s, i, *_: (s, 0, 0))
    whole = lambda v: pl.BlockSpec(v.shape, lambda s, i, *_: (0,) * v.ndim)
    return rows, per_slot, whole


def up_and_down(live, mixture, tokens, cotangent, added, gains, w_proj, w_up, w_down):
    slots, length, width = tokens.shape
    hidden = w_up[1][1]
    block = row_block(length, 272)
    chunk = min(512, hidden)
    held = Weights([w_proj, w_up, w_down])
    n_held = len(held.refs)

    def kernel(starts_ref, live_ref, o_ref, x_ref, c_ref, e_ref, g_ref, *rest):
        refs = rest[:n_held]
        a_ref, f_ref, du_ref, dm_ref, z_ref, h_ref, out_ref, sum_ref = rest[n_held : n_held + 8]
        wp, wu, wd = rest[n_held + 8 : n_held + 11]
        slope_ref = rest[n_held + 12]

        @pl.when((pl.program_id(0) == 0) & (pl.program_id(1) == 0))
        def _():
            copies = held.copies(starts_ref, refs, rest[n_held + 8 : n_held + 12])
            for some in copies:
                run_all(some, "start")
            for some in copies:
                run_all(some, "wait")

        @pl.when(pl.program_id(1) == 0)
        def _():
            sum_ref[...] = jnp.zeros_like(sum_ref)

        alive = live_ref[pl.program_id(0)].astype(jnp.float32)
        parts = halves(block)
        cols = [slice(j, j + chunk) for j in range(0, hidden, chunk)]
        h1, a, m, dm = {}, {}, {}, {}
        zs = [dot(o_ref[0, r, :], wp[...], 1, 0) for r in parts]

        def enter(n):
            r = parts[n]
            z_ref[0, r, :] = zs[n]
            h1[n] = x_ref[0, r, :] + e_ref[0] + normed(zs[n])[0] * g_ref[1:2]
            h_ref[0, r, :] = h1[n]
            a[n] = (normed(h1[n])[0] * g_ref[2:3]).astype(jnp.bfloat16)
            a_ref[0, r, :] = a[n]

        def leave(n):
            r = parts[n]
            unit_m, inv_m = normed(m[n])
            out_ref[0, r, :] = alive * (h1[n] + unit_m * g_ref[3:4])
            dy = alive * c_ref[0, r, :]
            dm[n] = norm_back(dy, unit_m, inv_m, g_ref[3:4]).astype(jnp.bfloat16)
            dm_ref[0, r, :] = dm[n]
            sum_ref[0, 0:1] += jnp.sum(dy * unit_m, axis=0, keepdims=True)

        def raised(job):
            n, c = job
            u = dot(a[n], wu[:, c], 1, 0)
            if c is cols[1 % len(cols)] and n + 1 < len(parts):
                enter(n + 1)
            return u

        def activate(job, u):
            n, c = job
            f, slope = gelu_parts(u)
            f_ref[0, parts[n], c] = f.astype(jnp.bfloat16)
            slope_ref[parts[n], c] = slope.astype(jnp.bfloat16)
            return f.astype(jnp.bfloat16)

        def lower(job, f):
            n, c = job
            more = dot(f, wd[c, :], 1, 0)
            m[n] = m[n] + more if n in m else more
            if c is cols[-1]:
                leave(n)

        enter(0)
        staged([(n, c) for n in range(len(parts)) for c in cols], raised, activate, lower)
        dm = jnp.concatenate([dm[n] for n in range(len(parts))], axis=0)

        def lift(cols, df):
            du_ref[0, :, cols] = (df * slope_ref[:, cols].astype(jnp.float32)).astype(jnp.bfloat16)

        staged(cols, lambda c: dot(dm, wd[c, :], 1, 1), lift, lambda c, _: None)

    rows, per_slot, whole = token_specs(tokens.shape, block)
    wide = pl.BlockSpec((1, block, hidden), lambda s, i, *_: (s, i, 0))
    low = jax.ShapeDtypeStruct(tokens.shape, jnp.bfloat16)
    low_wide = jax.ShapeDtypeStruct((slots, length, hidden), jnp.bfloat16)
    full = jax.ShapeDtypeStruct(tokens.shape, jnp.float32)
    return pl.pallas_call(
        kernel,
        grid_spec=pltpu.PrefetchScalarGridSpec(
            num_scalar_prefetch=2,
            grid=(slots, length // block),
            in_specs=[rows, rows, rows, per_slot(1), whole(gains)] + held.in_specs,
            out_specs=[rows, wide, wide, rows, rows, rows, rows, per_slot(8)],
            scratch_shapes=held.scratch + [pltpu.VMEM((block, hidden), jnp.bfloat16)],
        ),
        out_shape=[low, low_wide, low_wide, low, full, full, full, jax.ShapeDtypeStruct((slots, 8, width), jnp.float32)],
        compiler_params=params(),
        name="up_and_down",
    )(held.starts, live, mixture, tokens, cotangent, added, gains, *held.refs)


def back_to_mixture(live, du, h1, z, cotangent, gains, w_proj, w_up):
    slots, length, width = h1.shape
    hidden = du.shape[-1]
    block = row_block(length, 272)
    held = Weights([w_up, w_proj])
    n_held = len(held.refs)

    def kernel(starts_ref, live_ref, du_ref, h_ref, z_ref, c_ref, g_ref, *rest):
        refs = rest[:n_held]
        dz_ref, do_ref, dh_ref, sum_ref = rest[n_held : n_held + 4]
        wu, wp = rest[n_held + 4 : n_held + 6]

        @pl.when((pl.program_id(0) == 0) & (pl.program_id(1) == 0))
        def _():
            copies = held.copies(starts_ref, refs, rest[n_held + 4 : n_held + 7])
            for some in copies:
                run_all(some, "start")
            for some in copies:
                run_all(some, "wait")

        @pl.when(pl.program_id(1) == 0)
        def _():
            sum_ref[...] = jnp.zeros_like(sum_ref)

        alive = live_ref[pl.program_id(0)].astype(jnp.float32)
        da = dot(du_ref[0], wu[...], 1, 1)
        unit_h, inv_h = normed(h_ref[0])
        unit_z, inv_z = normed(z_ref[0])
        dh1 = alive * c_ref[0] + norm_back(da, unit_h, inv_h, g_ref[2:3])
        dh_ref[0] = dh1
        dz = norm_back(dh1, unit_z, inv_z, g_ref[1:2]).astype(jnp.bfloat16)
        dz_ref[0] = dz
        do_ref[0] = dot(dz, wp[...], 1, 1).astype(jnp.bfloat16)
        sum_ref[0, 0:1] += jnp.sum(dh1 * unit_z, axis=0, keepdims=True)
        sum_ref[0, 1:2] += jnp.sum(da * unit_h, axis=0, keepdims=True)

    rows, per_slot, whole = token_specs(h1.shape, block)
    wide = pl.BlockSpec((1, block, hidden), lambda s, i, *_: (s, i, 0))
    low = jax.ShapeDtypeStruct(h1.shape, jnp.bfloat16)
    return pl.pallas_call(
        kernel,
        grid_spec=pltpu.PrefetchScalarGridSpec(
            num_scalar_prefetch=2,
            grid=(slots, length // block),
            in_specs=[wide, rows, rows, rows, whole(gains)] + held.in_specs,
            out_specs=[rows, rows, rows, per_slot(8)],
            scratch_shapes=held.scratch,
        ),
        out_shape=[
            low,
            low,
            jax.ShapeDtypeStruct(h1.shape, jnp.float32),
            jax.ShapeDtypeStruct((slots, 8, width), jnp.float32),
        ],
        compiler_params=params(),
        name="back_to_mixture",
    )(held.starts, live, du, h1, z, cotangent, gains, *held.refs)


def project_back(slot, part_of, groups, tokens, grad_middle, added, gain, weights, before=None):
    slots, length, width = tokens.shape
    block = row_block(length // part_of[1], 272)
    held = Weights(weights)
    per_weight = len(groups) // len(weights)
    n_held = len(held.refs)
    n_before = 0 if before is None else 2

    n_groups, part = len(groups), groups[0].shape[-1]
    steps = length // part_of[1] // block
    skip = part_of[0] * steps

    def kernel(starts_ref, *refs_in):
        d_refs, (x_ref, h_ref, e_ref, g_ref), rest = refs_in[:n_groups], refs_in[n_groups : n_groups + 4], refs_in[n_groups + 4 :]
        refs, rest = rest[:n_held], rest[n_held + n_before :]
        (out_ref, sum_ref), scratch = rest[:2], rest[2:]
        first = pl.program_id(0) == 0
        copies = sum(held.copies(starts_ref, refs, scratch), [])

        @pl.when(first)
        def _():
            run_all(copies, "start")

        unit, inv_std = normed(x_ref[0] + e_ref[0])

        @pl.when(first)
        def _():
            run_all(copies, "wait")

        da = None
        for w in range(len(weights)):
            mine = d_refs[w * per_weight : (w + 1) * per_weight]
            for i in range(3):
                more = dot(jnp.concatenate([ref[i, 0] for ref in mine], axis=1), scratch[w][i], 1, 1)
                da = more if da is None else da + more
        dh = h_ref[0] + norm_back(da, unit, inv_std, g_ref[...])
        out_ref[0] = dh

        @pl.when(pl.program_id(0) == 0)
        def _():
            sum_ref[...] = jnp.zeros_like(sum_ref)

        sum_ref[0, 0:1] += jnp.sum(da * unit, axis=0, keepdims=True)
        sum_ref[0, 1:2] += jnp.sum(dh, axis=0, keepdims=True)

    rows = pl.BlockSpec((1, block, width), lambda i, _: (slot, skip + i, 0))
    return pl.pallas_call(
        kernel,
        grid_spec=pltpu.PrefetchScalarGridSpec(
            num_scalar_prefetch=1,
            grid=(steps,),
            in_specs=[pl.BlockSpec((3, 1, block, part), lambda i, _: (0, slot, skip + i, 0))] * n_groups
            + [
                rows,
                rows,
                pl.BlockSpec((1, 1, width), lambda i, _: (slot, 0, 0)),
                pl.BlockSpec((1, width), lambda i, _: (0, 0)),
            ]
            + held.in_specs
            + [pl.BlockSpec(memory_space=pl.ANY)] * n_before,
            out_specs=[
                rows,
                pl.BlockSpec((1, 8, width), lambda i, _: (slot * 2 + part_of[0], 0, 0)),
            ],
            scratch_shapes=held.scratch,
        ),
        out_shape=[
            jax.ShapeDtypeStruct(tokens.shape, jnp.float32),
            jax.ShapeDtypeStruct((slots * 2, 8, width), jnp.float32),
        ],
        input_output_aliases={5 + n_groups + n_held + i: i for i in range(n_before)},
        compiler_params=params(),
        name="project_back",
    )(held.starts, *groups, tokens, grad_middle, added, gain, *held.refs, *(before or ()))


def columns_of(refs):
    if len(refs[0].shape) == 3:
        return jnp.concatenate([ref[0] for ref in refs], axis=1)
    return refs[0][...]


def grad_blocks(order, left, right, received=None):
    rows, depth = left.shape[0], left.shape[1] // 4
    tall = min(depth, 512)
    per_block = depth // tall
    stacked = isinstance(right, list)
    if stacked:
        count, slab = right[0].shape[0], sum(r.shape[-1] for r in right)
        right_specs = [pl.BlockSpec((1, rows, r.shape[-1]), lambda r, k, j, order: (j, 0, 0)) for r in right]
    else:
        slab = min(1024, right.shape[1])
        count = right.shape[1] // slab
        right_specs = [pl.BlockSpec((rows, slab), lambda r, k, j, order: (0, j))]
        right = [right]
    n_right = len(right)
    if depth <= 512:
        return narrow_grad_blocks(order, left, right, right_specs, (count, depth, slab), received)

    def kernel(order_ref, a_ref, *rest):
        right_block = columns_of(rest[:n_right])
        outs = rest[n_right:]
        total = dot(a_ref[...], right_block, 0, 0)
        if received is None:
            outs[0][0, 0] = total.astype(jnp.bfloat16)
            return
        total = (total + outs[0][0, 0].astype(jnp.float32)).astype(jnp.bfloat16)

        @pl.when(pl.program_id(0) == 0)
        def _():
            outs[1][0] = total

        @pl.when(pl.program_id(0) == 1)
        def _():
            outs[2][0] = total

    both = pl.BlockSpec((1, 1, tall, slab), lambda r, k, j, order: (r, j, k, 0))
    sent = pl.BlockSpec((1, tall, slab), lambda r, k, j, order: (jnp.where(r == 0, j, count - 1), jnp.where(r == 0, k, per_block - 1), 0))
    kept = pl.BlockSpec((1, tall, slab), lambda r, k, j, order: (jnp.where(r == 0, 0, j), jnp.where(r == 0, 0, k), 0))
    more = [] if received is None else [received]
    shape = (count, depth, slab)
    return pl.pallas_call(
        kernel,
        grid_spec=pltpu.PrefetchScalarGridSpec(
            num_scalar_prefetch=1,
            grid=(2, per_block, count),
            in_specs=[pl.BlockSpec((rows, tall), lambda r, k, j, order: (0, order[r] * per_block + k))]
            + right_specs
            + [both] * len(more),
            out_specs=[sent, kept] if more else both,
        ),
        out_shape=[jax.ShapeDtypeStruct(shape, jnp.bfloat16)] * 2 if more else jax.ShapeDtypeStruct((2,) + shape, jnp.bfloat16),
        compiler_params=params(),
        name="grad_blocks",
    )(order, left, *right, *more)


def narrow_grad_blocks(order, left, right, right_specs, shape, received):
    count, depth, slab = shape
    rows, n_right = left.shape[0], len(right)

    def kernel(order_ref, a0_ref, a1_ref, *rest):
        right_block = columns_of(rest[:n_right])
        outs = rest[n_right:]
        for r, a_ref in enumerate((a0_ref, a1_ref)):
            total = dot(a_ref[...], right_block, 0, 0)
            if received is None:
                outs[0][r, 0] = total.astype(jnp.bfloat16)
            else:
                outs[1 + r][0] = (total + outs[0][r, 0].astype(jnp.float32)).astype(jnp.bfloat16)

    by_step = lambda spec: pl.BlockSpec(spec.block_shape, lambda j, order: spec.index_map(0, 0, j, order))
    both = pl.BlockSpec((2, 1, depth, slab), lambda j, order: (0, j, 0, 0))
    one = pl.BlockSpec((1, depth, slab), lambda j, order: (j, 0, 0))
    left_spec = lambda r: pl.BlockSpec((rows, depth), lambda j, order: (0, order[r]), pipeline_mode=pl.Buffered(1))
    more = [] if received is None else [received]
    return pl.pallas_call(
        kernel,
        grid_spec=pltpu.PrefetchScalarGridSpec(
            num_scalar_prefetch=1,
            grid=(count,),
            in_specs=[left_spec(0), left_spec(1)] + [by_step(spec) for spec in right_specs] + [both] * len(more),
            out_specs=[one, one] if more else both,
        ),
        out_shape=[jax.ShapeDtypeStruct(shape, jnp.bfloat16)] * 2 if more else jax.ShapeDtypeStruct((2,) + shape, jnp.bfloat16),
        compiler_params=params(),
        name="grad_blocks",
    )(order, left, left, *right, *more)


def after(value, *earlier):
    return lax.optimization_barrier((value,) + earlier)[0]


def swap(value, axis, bit):
    size = lax.axis_size(axis)
    return lax.ppermute(value, axis, [(i, i ^ (1 << bit)) for i in range(size)])


def bit_of(axis, bit):
    return (lax.axis_index(axis) >> bit) & 1


def bits_of(axis):
    return range(lax.axis_size(axis).bit_length() - 1)


def pick(value, index):
    return lax.dynamic_index_in_dim(value, index, 0, keepdims=False)


def paired():
    return lax.axis_size("fsdp") == 2 and lax.axis_size("dp") % 2 == 0


def slot(before, ends=(), starts=()):
    before = tuple(before)
    if not paired():
        for e in ends:
            e.take()
        return before
    if ends:
        arrived = lax.optimization_barrier(tuple(e.received for e in ends) + before)
        for e, value in zip(ends, arrived):
            e.received = value
            e.take()
        before = arrived[len(ends) :]
    if starts:
        leaving = lax.optimization_barrier(tuple(e.sent for e in starts) + before)
        for e, value in zip(starts, leaving):
            e.send(value)
        before = leaving
    return before


class Gather:
    def __init__(self, low, ranges=None):
        self.low, self.ranges = low, ranges
        self.size, wide = low.shape
        whole = self.size * lax.axis_size("fsdp")
        self.shape = (whole, wide) if ranges is None else (len(ranges), whole, ranges[0][1] - ranges[0][0])
        self.crossed = None
        if paired():
            half = self.size // 2
            mine = lambda lo, hi: lax.dynamic_slice(low, (bit_of("dp", 0) * half, lo), (half, hi - lo))
            self.sent = mine(0, wide) if ranges is None else jnp.stack([mine(lo, hi) for lo, hi in ranges])
        else:
            self.sent = low

    def send(self, value):
        self.received = swap(value, "fsdp" if self.crossed is None else "dp", 0)

    def take(self):
        if not paired():
            return
        if self.crossed is None:
            self.crossed = self.sent = self.received
        else:
            self.beside = self.received

    def parts(self):
        ranges = () if self.ranges is None else (self.ranges,)
        if not paired():
            return [(lax.all_gather(self.low, "fsdp", axis=0, tiled=True), 0) + ranges], self.shape
        size, c, x = self.size, bit_of("dp", 0), lax.axis_index("fsdp")
        base = (1 - x) * size
        own = (self.low, x * size) + ranges
        return [own, (self.crossed, base + c * (size // 2)), (self.beside, base + (1 - c) * (size // 2))], self.shape


class WideGather:
    def __init__(self, low):
        self.low = low
        self.shape = (low.shape[0] * lax.axis_size("fsdp"), low.shape[1])
        self.crossed = None
        self.sent = low
        if paired():
            n_dp = lax.axis_size("dp")
            self.sent = pick(low.reshape(n_dp, low.shape[0] // n_dp, low.shape[1]), lax.axis_index("dp"))

    def send(self, value):
        if self.crossed is None:
            self.received = swap(value, "fsdp", 0)
        else:
            self.other = lax.all_gather(value, "dp", axis=0, tiled=True)

    def take(self):
        if paired():
            self.crossed = self.sent = self.received

    def parts(self):
        if not paired():
            return [(lax.all_gather(self.low, "fsdp", axis=0, tiled=True), 0)], self.shape
        size, x = self.low.shape[0], lax.axis_index("fsdp")
        return [(self.low, x * size), (self.other, (1 - x) * size)], self.shape


class Columns:
    def __init__(self, low):
        self.low = self.sent = low

    def send(self, value):
        self.received = swap(value, "fsdp", 0)

    def take(self):
        if not paired():
            self.whole = lax.all_gather(self.low, "fsdp", axis=1, tiled=True)
            return
        first = lax.axis_index("fsdp") == 0
        self.whole = jnp.concatenate(
            [jnp.where(first, self.low, self.received), jnp.where(first, self.received, self.low)], axis=1
        )


class SmallSum:
    def __init__(self, value):
        self.value, self.bits = value, None
        if paired():
            halves = value.reshape(value.shape[0], 2, -1)
            x = lax.axis_index("fsdp")
            self.value = lax.dynamic_index_in_dim(halves, x, 1, keepdims=False)
            self.sent = lax.dynamic_index_in_dim(halves, 1 - x, 1, keepdims=False)

    def send(self, value):
        if self.bits is None:
            self.bits = list(bits_of("dp"))
            self.received = swap(value, "fsdp", 0)
        else:
            self.received = swap(value, "dp", self.bits.pop(0))

    def take(self):
        if paired():
            self.value = self.sent = self.value + self.received

    def result(self):
        if paired():
            return self.value
        return lax.psum(lax.psum_scatter(self.value, "fsdp", scatter_dimension=1, tiled=True), "dp")


def assemble(pieces):
    count, rows, wide = pieces[0][0].shape
    n_pieces = len(pieces)

    def kernel(c_ref, *refs):
        out_ref = refs[-1]
        for p in range(n_pieces):

            @pl.when(pl.program_id(1) == p)
            def _():
                for i, ref in enumerate(refs[2 * p : 2 * p + 2]):
                    half = c_ref[0] if i == 0 else 1 - c_ref[0]
                    out_ref[pl.ds(pl.multiple_of(half * rows, rows), rows), :] = ref[0].astype(jnp.float32)

    return pl.pallas_call(
        kernel,
        grid_spec=pltpu.PrefetchScalarGridSpec(
            num_scalar_prefetch=1,
            grid=(count, n_pieces),
            in_specs=[pl.BlockSpec((1, rows, wide), lambda i, p, c: (i, 0, 0))] * (2 * n_pieces),
            out_specs=pl.BlockSpec((2 * rows, wide), lambda i, p, c: (0, i * n_pieces + p)),
        ),
        out_shape=jax.ShapeDtypeStruct((2 * rows, count * n_pieces * wide), jnp.float32),
        compiler_params=params(),
        name="assemble",
    )(bit_of("dp", 0).astype(jnp.int32).reshape(1), *[v for piece in pieces for v in piece])


def in_rows(whole):
    n, count, rows, wide = whole.shape
    n_bits = n.bit_length() - 1
    step = min(wide, 512)

    def place(i):
        return sum(((i >> (n_bits - 1 - b)) & 1) << b for b in range(n_bits))

    def kernel(in_ref, out_ref):
        for i in range(n):
            out_ref[place(i) * rows : (place(i) + 1) * rows, :] = in_ref[i, 0].astype(jnp.float32)

    return pl.pallas_call(
        kernel,
        grid=(count, wide // step),
        in_specs=[pl.BlockSpec((n, 1, rows, step), lambda s, j: (0, s, 0, j))],
        out_specs=pl.BlockSpec((n * rows, step), lambda s, j: (0, s * (wide // step) + j)),
        out_shape=jax.ShapeDtypeStruct((n * rows, count * wide), jnp.float32),
        compiler_params=params(),
        name="in_rows",
    )(whole)


class GradSum:
    def __init__(self, left, right, spread=False):
        self.left, self.right, self.spread = left, right, spread
        self.state = "send"
        if paired():
            self.bits = list(bits_of("dp"))[1:]

    def part(self, before):
        if not paired():
            if self.state == "send":
                right = self.right
                if isinstance(right, list):
                    right = jnp.concatenate([r[i] for i in range(3) for r in right], axis=1)
                low = dot(self.left, right, 0, 0).astype(jnp.bfloat16)
                piece = lax.psum_scatter(low, ("fsdp", "dp"), scatter_dimension=0, tiled=True)
                self.total = lax.all_gather(piece, "dp", axis=0, tiled=True).astype(jnp.float32)
                self.state = "keep"
            return before
        c, x = bit_of("dp", 0), lax.axis_index("fsdp")
        left = after(self.left, *before)
        if self.state == "send":
            order = jnp.stack([(1 - x) * 2 + 1 - c, x * 2 + 1 - c]).astype(jnp.int32)
            self.sent = grad_blocks(order, left, self.right)
        else:
            order = jnp.stack([(1 - x) * 2 + c, x * 2 + c]).astype(jnp.int32)
            self.sent, self.kept = grad_blocks(order, left, self.right, self.received)
        return (self.sent,)

    def send(self, value):
        if self.state == "send":
            self.received = swap(value, "dp", 0)
        elif self.state == "keep":
            self.received = swap(value, "fsdp", 0)
        elif self.state == "halve":
            self.received = swap(value, "dp", self.bit)
        elif self.spread:
            self.whole = lax.all_gather(value, "dp", axis=0, tiled=False)
        else:
            self.received = swap(value, "dp", self.bit)

    def take(self):
        if not paired():
            return
        if self.state == "send":
            self.state = "keep"
        elif self.state in ("keep", "halve"):
            if self.bits:
                self.state, self.bit = "halve", self.bits.pop(0)
                b = bit_of("dp", self.bit)
                slabs, rows, wide = self.kept.shape
                kept, received = (v.reshape(slabs, 2, rows // 2, wide) for v in (self.kept, self.received))
                part = lambda v, i: lax.dynamic_index_in_dim(v, i, 1, keepdims=False).astype(jnp.float32)
                self.sent = (part(kept, 1 - b) + part(received, 1 - b)).astype(jnp.bfloat16)
                self.kept = (part(kept, b) + part(received, b)).astype(jnp.bfloat16)
            else:
                self.kept = self.sent = (self.kept.astype(jnp.float32) + self.received.astype(jnp.float32)).astype(jnp.bfloat16)
                self.state, self.bits = "join", list(bits_of("dp"))
                self.bit = self.bits.pop()
        elif self.bits:
            self.kept = self.sent = in_order(self.kept, self.received, bit_of("dp", self.bit))
            self.bit = self.bits.pop()
        else:
            self.state = "done"

    def result(self, *earlier):
        if not paired():
            return self.total
        if self.spread:
            return in_rows(after(self.whole, *earlier))
        return assemble([(after(self.kept, *earlier), self.received)])


def in_order(mine, other, bit):
    return jnp.where(bit == 0, jnp.concatenate([mine, other], axis=1), jnp.concatenate([other, mine], axis=1))


def local(tokens, cotangent, group_ids, counts, w_qkv, w_proj, w_up, w_down, gains, table):
    slots, length, width = tokens.shape
    rows = slots * length
    flat = lambda v: v.reshape(v.shape[:-3] + (rows, v.shape[-1]))
    pairs = width // LANES
    n_groups = 2
    group_pairs = pairs // n_groups
    half = group_pairs // 2
    part = width // n_groups
    small = Columns(jnp.concatenate([gains, table], axis=0).astype(jnp.bfloat16))
    low_qkv = w_qkv.astype(jnp.bfloat16)
    get_qkv = [
        Gather(low_qkv, [(i * width + j * part, i * width + (j + 1) * part) for i in range(3)]) for j in range(n_groups)
    ]
    t = slot((), starts=[small, get_qkv[0]])
    get_down = WideGather(after(w_down, *t).astype(jnp.bfloat16))
    get_proj = Gather(after(w_proj, *t).astype(jnp.bfloat16))
    get_up = Gather(after(w_up, *t).astype(jnp.bfloat16))
    t = (get_down.sent, get_proj.sent, get_up.sent)
    t = slot(t, [small])
    small = small.whole.astype(jnp.float32)
    g = small[: gains.shape[0]]
    embed = small[gains.shape[0] :]
    onehot = (group_ids[:, None] == jnp.arange(table.shape[0])[None, :]).astype(jnp.float32)
    added = jnp.sum(onehot[:, :, None] * embed[None], axis=1)[:, None, :]
    live = (jnp.arange(slots) < counts[0]).astype(jnp.int32)
    a1 = norm_in(after(tokens, *t), added, g[0:1])
    t = slot((a1,), [get_qkv[0]], [get_qkv[0], get_qkv[1], get_down])
    t = slot(t, [get_qkv[0]])

    qkv = []
    group = project_in(after(a1, *t), get_qkv[0].parts())
    qkv.append(group)
    t = slot((group,), [get_qkv[1], get_down], [get_qkv[1], get_down, get_up, get_proj])
    attended = attn_fwd(after(group, *t), 0, group_pairs, 0, width)
    t = slot((attended[0],), [get_qkv[1]])
    group = project_in(after(a1, *t), get_qkv[1].parts())
    qkv.append(group)
    mixture, log_totals = attn_fwd(group, 0, group_pairs, group_pairs, width, attended)
    t = slot((mixture,), [get_up, get_proj], [get_up, get_proj])
    t = slot(t, [get_up, get_proj])
    p_qkv = [w.parts() for w in get_qkv]
    p_proj, p_up, p_down = get_proj.parts(), get_up.parts(), get_down.parts()
    a3, f, du, dm, z, h1, output, sums_out = up_and_down(
        live, after(mixture, *t), tokens, cotangent, added, g, p_proj, p_up, p_down
    )

    down = GradSum(flat(f), flat(dm), spread=True)
    up = GradSum(flat(a3), flat(du), spread=True)
    t = slot(down.part((dm,)), [], [down])
    t = slot(up.part(t), [down], [up])
    t = slot(down.part(t), [up], [down])
    t = up.part(t)
    dz, do, dh1, sums_mid = back_to_mixture(live, after(du, *t), h1, z, cotangent, g, p_proj, p_up)
    t = slot((dz,), [down], [down, up])
    proj = GradSum(flat(mixture), flat(dz))
    t = slot(proj.part(t), [], [proj])
    chunks = []

    def attend(i, t):
        group = i // 2
        chunks.append(attn_bwd(qkv[group], mixture, after(do, *t), log_totals, (i % 2) * half, half, group * group_pairs))
        return (chunks[-1],)

    t = attend(0, t)
    t = slot(t, [down, proj], [down])
    t = slot(proj.part(t), [], [proj])
    t = attend(1, t)
    t = slot(t, [up, down, proj], [up, down, proj])
    first = GradSum(flat(a1), [flat(d) for d in chunks])
    t = slot(first.part(t), [proj], [first, proj])
    t = attend(2, t)
    t = slot(t, [up, down, first, proj], [up, down, proj])
    t = slot(first.part(t), [proj], [first, proj])
    t = attend(3, t)
    t = slot(t, [up, first, proj], [up, first, proj])
    last = GradSum(flat(a1), [flat(d) for d in chunks[2:]])
    t = slot(last.part(t), [proj], [last, proj])
    grad_down = down.result(*t)
    t = slot((grad_down,), [last])
    t = slot(last.part(t), [up, first, proj], [up, last, first, proj])
    back = project_back(0, (0, 1), chunks, tokens, after(dh1, *t), added, g[0:1], p_qkv)
    t = slot((back[0],), [last, first, proj], [last, first])
    back = project_back(1, (0, 2), chunks, tokens, after(dh1, *t), added, g[0:1], p_qkv, back)
    t = slot((back[0],), [last, first], [last, first])
    back = project_back(1, (1, 2), chunks, tokens, after(dh1, *t), added, g[0:1], p_qkv, back)
    grad_tokens, more = back
    more = jnp.stack([more[0], more[2] + more[3]])
    grad_embed = jnp.sum(onehot[:, :, None] * more[:, None, 1, :], axis=0)
    grad_gains = jnp.concatenate([more[:, 0:1], sums_mid[:, 0:2], sums_out[:, 0:1]], axis=1).sum(axis=0)
    little = SmallSum(jnp.concatenate([grad_gains, grad_embed], axis=0))
    t = slot((more, little.sent) if paired() else (more,), [last, first], [last, first, little])
    grad_proj = proj.result(*t)
    t = slot((grad_proj,), [last, first, little], [last, first, little])
    grad_up = up.result(*t)
    t = (grad_up,)
    waiting = [last, first, little]
    while paired() and last.state != "done":
        t = slot(t, waiting)
        waiting = [e for e in (last, first) if e.state != "done"] + ([little] if little.bits else [])
        if waiting:
            t = slot(t, [], waiting)
    if paired():
        grad_qkv = assemble([(e.kept, e.received) for e in (first, last)])
    else:
        part = first.total.shape[1] // 3
        grad_qkv = jnp.concatenate([e.total[:, i * part : (i + 1) * part] for i in range(3) for e in (first, last)], axis=1)
    small_sum = little.result()
    return (
        output,
        grad_tokens,
        grad_qkv,
        grad_proj,
        grad_up,
        grad_down,
        small_sum[: gains.shape[0]],
        small_sum[gains.shape[0] :],
    )


def solution(mesh):
    by_seq = P(("dp", "fsdp"), None, None)
    by_slot = P(("dp", "fsdp"))
    by_row = P("fsdp", None)
    by_col = P(None, "fsdp")
    return jax.shard_map(
        local,
        mesh=mesh,
        in_specs=(by_seq, by_seq, by_slot, by_slot) + (by_row,) * 4 + (by_col,) * 2,
        out_specs=(by_seq, by_seq) + (by_row,) * 4 + (by_col,) * 2,
        check_vma=False,
    )
```

```python
import math

import jax
import jax.numpy as jnp
from jax import lax
from jax.experimental import pallas as pl
from jax.experimental.pallas import tpu as pltpu
from jax.sharding import PartitionSpec as P

HEAD_DIM = 64
LANES = 128
EPSILON = 1e-05
NEG = -1e30
ATTN_ROWS = 256
VMEM_BYTES = 60 * 1024 * 1024


def dot(a, b, a_dim, b_dim):
    return lax.dot_general(a, b, (((a_dim,), (b_dim,)), ((), ())), preferred_element_type=jnp.float32)


def params(*semantics):
    return pltpu.CompilerParams(vmem_limit_bytes=VMEM_BYTES)


def row_block(length, most):
    return max(b for b in range(16, most + 1, 16) if length % b == 0)


def normed(rows):
    centered = rows - jnp.mean(rows, axis=-1, keepdims=True)
    inv_std = lax.rsqrt(jnp.mean(centered * centered, axis=-1, keepdims=True) + EPSILON)
    return centered * inv_std, inv_std


def halves(rows):
    middle = rows // 32 * 16
    return [slice(0, middle), slice(middle, rows)] if middle else [slice(0, rows)]


def norm_back(gradient, unit, inv_std, gain):
    grad_unit = gradient * gain
    first = jnp.mean(grad_unit, axis=-1, keepdims=True)
    second = jnp.mean(grad_unit * unit, axis=-1, keepdims=True)
    return inv_std * (grad_unit - first - unit * second)


def gelu_parts(u):
    cdf = 0.5 + 0.5 * lax.erf(u * math.sqrt(0.5))
    return u * cdf, cdf + u * jnp.exp(-0.5 * u * u) * (1.0 / math.sqrt(2.0 * math.pi))


def staged(jobs, one, two, three):
    n, firsts, seconds = len(jobs), {}, {}
    for i in range(n + 2):
        if i < n:
            firsts[i] = one(jobs[i])
        if i >= 2:
            three(jobs[i - 2], seconds.pop(i - 2))
        if 1 <= i <= n:
            seconds[i - 1] = two(jobs[i - 1], firsts.pop(i - 1))


def spans(length):
    return [(s, min(s + ATTN_ROWS, length)) for s in range(0, length, ATTN_ROWS)]


class Weights:
    def __init__(self, matrices):
        self.refs = [part[0] for parts, _ in matrices for part in parts]
        self.parts = [[part[1:] for part in parts] for parts, _ in matrices]
        self.shapes = [shape for _, shape in matrices]
        self.starts = jnp.stack([jnp.asarray(part[1], jnp.int32) for parts, _ in matrices for part in parts])
        self.in_specs = [pl.BlockSpec(memory_space=pl.ANY)] * len(self.refs)
        self.scratch = [pltpu.VMEM(shape, jnp.bfloat16) for shape in self.shapes]
        n_copies = sum(len(part[1]) if len(part) > 1 else 1 for parts in self.parts for part in parts)
        self.scratch.append(pltpu.SemaphoreType.DMA((n_copies,)))

    def copies(self, starts_ref, refs, scratch):
        lists, at, n = [], 0, 0
        for parts, whole in zip(self.parts, scratch[:-1]):
            mine = []
            for part in parts:
                rows = pl.ds(pl.multiple_of(starts_ref[at], 16), refs[at].shape[-2])
                pairs = [(refs[at], whole.at[..., rows, :])]
                if len(part) > 1:
                    pairs = [(refs[at].at[:, lo:hi], whole.at[i, rows, :]) for i, (lo, hi) in enumerate(part[1])]
                for source, target in pairs:
                    mine.append(pltpu.make_async_copy(source, target, scratch[-1].at[n]))
                    n += 1
                at += 1
            lists.append(mine)
        return lists


def run_all(copies, method):
    for copy in copies:
        getattr(copy, method)()


def norm_in(tokens, added, gain):
    slots, length, width = tokens.shape
    block = row_block(length, 544)

    def kernel(x_ref, e_ref, g_ref, a_ref):
        a_ref[0] = (normed(x_ref[0] + e_ref[0])[0] * g_ref[...]).astype(jnp.bfloat16)

    rows = pl.BlockSpec((1, block, width), lambda s, i: (s, i, 0))
    return pl.pallas_call(
        kernel,
        grid=(slots, length // block),
        in_specs=[rows, pl.BlockSpec((1, 1, width), lambda s, i: (s, 0, 0)), pl.BlockSpec((1, width), lambda s, i: (0, 0))],
        out_specs=rows,
        out_shape=jax.ShapeDtypeStruct(tokens.shape, jnp.bfloat16),
        compiler_params=params(),
        name="norm_in",
    )(tokens, added, gain)


def project_in(a1, weight):
    slots, length, width = a1.shape
    part = weight[1][2]
    block = row_block(length, 544)
    held = Weights([weight])
    n_held = len(held.refs)

    def kernel(starts_ref, a_ref, *rest):
        refs, out_ref, scratch = rest[:n_held], rest[n_held], rest[n_held + 1 :]

        @pl.when((pl.program_id(0) == 0) & (pl.program_id(1) == 0))
        def _():
            copies = held.copies(starts_ref, refs, scratch)[0]
            run_all(copies, "start")
            run_all(copies, "wait")

        for i in range(3):
            out_ref[i, 0] = dot(a_ref[0], scratch[0][i], 1, 0).astype(jnp.bfloat16)

    return pl.pallas_call(
        kernel,
        grid_spec=pltpu.PrefetchScalarGridSpec(
            num_scalar_prefetch=1,
            grid=(slots, length // block),
            in_specs=[pl.BlockSpec((1, block, width), lambda s, i, _: (s, i, 0))] + held.in_specs,
            out_specs=pl.BlockSpec((3, 1, block, part), lambda s, i, _: (0, s, i, 0)),
            scratch_shapes=held.scratch,
        ),
        out_shape=jax.ShapeDtypeStruct((3, slots, length, part), jnp.bfloat16),
        compiler_params=params(),
        name="project_in",
    )(held.starts, a1, *held.refs)


def causal(scores, keys_first):
    q = lax.broadcasted_iota(jnp.int32, scores.shape, 1 if keys_first else 0)
    k = lax.broadcasted_iota(jnp.int32, scores.shape, 0 if keys_first else 1)
    return q >= k


def attn_fwd_kernel(x_ref, o_ref, l_ref):
    length = x_ref.shape[2]
    first = lax.broadcasted_iota(jnp.int32, (1, LANES), 1) < HEAD_DIM
    jobs = [(lo, hi, h) for lo, hi in spans(length) for h in range(2)]
    outs = {}

    def scores(job):
        lo, hi, h = job
        q = x_ref[0, 0, lo:hi, :] * (1.0 / math.sqrt(HEAD_DIM))
        q = jnp.where(first if h == 0 else ~first, q, 0).astype(jnp.bfloat16)
        near = dot(q, x_ref[1, 0, lo:hi, :], 1, 1)
        near = jnp.where(causal(near, False), near, NEG)
        return near, dot(q, x_ref[1, 0, 0:lo, :], 1, 1) if lo else None

    def weights(job, both):
        near, far = both
        top = jnp.max(near, axis=1, keepdims=True)
        if far is not None:
            top = jnp.maximum(top, jnp.max(far, axis=1, keepdims=True))
        near = jnp.exp(near - top)
        if far is not None:
            far = jnp.exp(far - top).astype(jnp.bfloat16)
        return near.astype(jnp.bfloat16), far, top

    def with_ones(a, b):
        v = x_ref[2, 0, a:b, :]
        return jnp.concatenate([v, jnp.ones_like(v)], axis=1)

    def mix(job, parts):
        lo, hi, h = job
        near, far, top = parts
        o = dot(near, with_ones(lo, hi), 1, 0)
        if far is not None:
            o = o + dot(far, with_ones(0, lo), 1, 0)
        o, total = o[:, :LANES], o[:, LANES:]
        outs[h] = o / total
        log_total = top + jnp.log(total)
        l_ref[0, 0, h : h + 1, lo:hi] = jnp.transpose(log_total)[0:1, :]
        if h == 1:
            o_ref[0, lo:hi, :] = jnp.where(first, outs[0], outs[1]).astype(jnp.bfloat16)

    staged(jobs, scores, weights, mix)


def attn_fwd(qkv, start, count, first_pair, width, before=None):
    _, slots, length, _ = qkv.shape
    place = first_pair + start
    n_before = 0 if before is None else 2

    def kernel(x_ref, *rest):
        attn_fwd_kernel(x_ref, *rest[n_before:])

    return pl.pallas_call(
        kernel,
        grid=(slots, count),
        in_specs=[pl.BlockSpec((3, 1, length, LANES), lambda s, p: (0, s, 0, start + p))]
        + [pl.BlockSpec(memory_space=pl.ANY)] * n_before,
        out_specs=[
            pl.BlockSpec((1, length, LANES), lambda s, p: (s, 0, place + p)),
            pl.BlockSpec((1, 1, 2, length), lambda s, p: (s, place + p, 0, 0)),
        ],
        out_shape=[
            jax.ShapeDtypeStruct((slots, length, width), jnp.bfloat16),
            jax.ShapeDtypeStruct((slots, width // LANES, 2, length), jnp.float32),
        ],
        input_output_aliases={1 + i: i for i in range(n_before)},
        compiler_params=params(),
        name="attn_fwd",
    )(qkv, *(before or ()))


def attn_bwd_kernel(x_ref, o_ref, do_ref, l_ref, d_ref, dqt_ref):
    length = x_ref.shape[2]
    scale = 1.0 / math.sqrt(HEAD_DIM)
    first = lax.broadcasted_iota(jnp.int32, (1, LANES), 1) < HEAD_DIM
    q = x_ref[0, 0] * scale
    do = do_ref[0]
    prod = jnp.transpose(do.astype(jnp.float32) * o_ref[0].astype(jnp.float32))
    deltas = [jnp.sum(prod[:HEAD_DIM], axis=0, keepdims=True), jnp.sum(prod[HEAD_DIM:], axis=0, keepdims=True)]
    dqt_ref[...] = jnp.zeros_like(dqt_ref)
    jobs = []
    for lo, hi in spans(length):
        for h in range(2):
            jobs.append((lo, hi, h, lo, hi))
            if hi < length:
                jobs.append((lo, hi, h, hi, length))
    sums = {}

    def scores(job):
        lo, hi, h, a, b = job
        mine = lambda v: jnp.where(first if h == 0 else ~first, v, 0).astype(jnp.bfloat16)
        return dot(mine(x_ref[1, 0, lo:hi, :]), q[a:b], 1, 1), dot(mine(x_ref[2, 0, lo:hi, :]), do[a:b], 1, 1)

    def weights(job, both):
        lo, hi, h, a, b = job
        p = jnp.exp(both[0] - l_ref[0, 0, h : h + 1, a:b])
        if a == lo:
            p = jnp.where(causal(p, True), p, 0.0)
        p = p.astype(jnp.bfloat16)
        return p, p * (both[1] - deltas[h][:, a:b]).astype(jnp.bfloat16)

    def collect(job, parts):
        lo, hi, h, a, b = job
        p, ds = parts
        dv, dk = dot(p, do[a:b], 1, 0), dot(ds, q[a:b], 1, 0)
        sums[h] = (dk, dv) if a == lo else (sums[h][0] + dk, sums[h][1] + dv)
        lanes = slice(h * HEAD_DIM, (h + 1) * HEAD_DIM)
        kt = jnp.transpose(x_ref[1, 0, lo:hi, :].astype(jnp.float32)).astype(jnp.bfloat16)
        dqt_ref[lanes, a:b] += dot(kt[lanes], ds, 1, 0)
        if h == 1 and b == length:
            for i in range(2):
                d_ref[1 + i, 0, lo:hi, :] = jnp.where(first, sums[0][i], sums[1][i]).astype(jnp.bfloat16)

    staged(jobs, scores, weights, collect)
    d_ref[0, 0] = (jnp.transpose(dqt_ref[...]) * scale).astype(jnp.bfloat16)


def attn_bwd(qkv, mixture, grad_mix, log_totals, start, count, first_pair):
    _, slots, length, _ = qkv.shape
    place = first_pair + start
    triple = pl.BlockSpec((3, 1, length, LANES), lambda s, p: (0, s, 0, start + p))
    single = pl.BlockSpec((1, length, LANES), lambda s, p: (s, 0, place + p))
    return pl.pallas_call(
        attn_bwd_kernel,
        grid=(slots, count),
        in_specs=[triple, single, single, pl.BlockSpec((1, 1, 2, length), lambda s, p: (s, place + p, 0, 0))],
        out_specs=pl.BlockSpec((3, 1, length, LANES), lambda s, p: (0, s, 0, p)),
        out_shape=jax.ShapeDtypeStruct((3, slots, length, count * LANES), jnp.bfloat16),
        scratch_shapes=[pltpu.VMEM((LANES, length), jnp.float32)],
        compiler_params=params(),
        name="attn_bwd",
    )(qkv, mixture, grad_mix, log_totals)


def token_specs(shape, block):
    slots, length, width = shape
    rows = pl.BlockSpec((1, block, width), lambda s, i, *_: (s, i, 0))
    per_slot = lambda n: pl.BlockSpec((1, n, width), lambda s, i, *_: (s, 0, 0))
    whole = lambda v: pl.BlockSpec(v.shape, lambda s, i, *_: (0,) * v.ndim)
    return rows, per_slot, whole


def up_and_down(live, mixture, tokens, cotangent, added, gains, w_proj, w_up, w_down):
    slots, length, width = tokens.shape
    hidden = w_up[1][1]
    block = row_block(length, 272)
    chunk = min(512, hidden)
    held = Weights([w_proj, w_up, w_down])
    n_held = len(held.refs)

    def kernel(starts_ref, live_ref, o_ref, x_ref, c_ref, e_ref, g_ref, *rest):
        refs = rest[:n_held]
        a_ref, f_ref, du_ref, dm_ref, z_ref, h_ref, out_ref, sum_ref = rest[n_held : n_held + 8]
        wp, wu, wd = rest[n_held + 8 : n_held + 11]
        slope_ref = rest[n_held + 12]

        @pl.when((pl.program_id(0) == 0) & (pl.program_id(1) == 0))
        def _():
            copies = held.copies(starts_ref, refs, rest[n_held + 8 : n_held + 12])
            for some in copies:
                run_all(some, "start")
            for some in copies:
                run_all(some, "wait")

        @pl.when(pl.program_id(1) == 0)
        def _():
            sum_ref[...] = jnp.zeros_like(sum_ref)

        alive = live_ref[pl.program_id(0)].astype(jnp.float32)
        parts = halves(block)
        cols = [slice(j, j + chunk) for j in range(0, hidden, chunk)]
        h1, a, m, dm = {}, {}, {}, {}
        zs = [dot(o_ref[0, r, :], wp[...], 1, 0) for r in parts]

        def enter(n):
            r = parts[n]
            z_ref[0, r, :] = zs[n]
            h1[n] = x_ref[0, r, :] + e_ref[0] + normed(zs[n])[0] * g_ref[1:2]
            h_ref[0, r, :] = h1[n]
            a[n] = (normed(h1[n])[0] * g_ref[2:3]).astype(jnp.bfloat16)
            a_ref[0, r, :] = a[n]

        def leave(n):
            r = parts[n]
            unit_m, inv_m = normed(m[n])
            out_ref[0, r, :] = alive * (h1[n] + unit_m * g_ref[3:4])
            dy = alive * c_ref[0, r, :]
            dm[n] = norm_back(dy, unit_m, inv_m, g_ref[3:4]).astype(jnp.bfloat16)
            dm_ref[0, r, :] = dm[n]
            sum_ref[0, 0:1] += jnp.sum(dy * unit_m, axis=0, keepdims=True)

        def raised(job):
            n, c = job
            u = dot(a[n], wu[:, c], 1, 0)
            if c is cols[1 % len(cols)] and n + 1 < len(parts):
                enter(n + 1)
            return u

        def activate(job, u):
            n, c = job
            f, slope = gelu_parts(u)
            f_ref[0, parts[n], c] = f.astype(jnp.bfloat16)
            slope_ref[parts[n], c] = slope.astype(jnp.bfloat16)
            return f.astype(jnp.bfloat16)

        def lower(job, f):
            n, c = job
            more = dot(f, wd[c, :], 1, 0)
            m[n] = m[n] + more if n in m else more
            if c is cols[-1]:
                leave(n)

        enter(0)
        staged([(n, c) for n in range(len(parts)) for c in cols], raised, activate, lower)
        dm = jnp.concatenate([dm[n] for n in range(len(parts))], axis=0)

        def lift(cols, df):
            du_ref[0, :, cols] = (df * slope_ref[:, cols].astype(jnp.float32)).astype(jnp.bfloat16)

        staged(cols, lambda c: dot(dm, wd[c, :], 1, 1), lift, lambda c, _: None)

    rows, per_slot, whole = token_specs(tokens.shape, block)
    wide = pl.BlockSpec((1, block, hidden), lambda s, i, *_: (s, i, 0))
    low = jax.ShapeDtypeStruct(tokens.shape, jnp.bfloat16)
    low_wide = jax.ShapeDtypeStruct((slots, length, hidden), jnp.bfloat16)
    full = jax.ShapeDtypeStruct(tokens.shape, jnp.float32)
    return pl.pallas_call(
        kernel,
        grid_spec=pltpu.PrefetchScalarGridSpec(
            num_scalar_prefetch=2,
            grid=(slots, length // block),
            in_specs=[rows, rows, rows, per_slot(1), whole(gains)] + held.in_specs,
            out_specs=[rows, wide, wide, rows, rows, rows, rows, per_slot(8)],
            scratch_shapes=held.scratch + [pltpu.VMEM((block, hidden), jnp.bfloat16)],
        ),
        out_shape=[low, low_wide, low_wide, low, full, full, full, jax.ShapeDtypeStruct((slots, 8, width), jnp.float32)],
        compiler_params=params(),
        name="up_and_down",
    )(held.starts, live, mixture, tokens, cotangent, added, gains, *held.refs)


def back_to_mixture(live, du, h1, z, cotangent, gains, w_proj, w_up):
    slots, length, width = h1.shape
    hidden = du.shape[-1]
    block = row_block(length, 272)
    held = Weights([w_up, w_proj])
    n_held = len(held.refs)

    def kernel(starts_ref, live_ref, du_ref, h_ref, z_ref, c_ref, g_ref, *rest):
        refs = rest[:n_held]
        dz_ref, do_ref, dh_ref, sum_ref = rest[n_held : n_held + 4]
        wu, wp = rest[n_held + 4 : n_held + 6]

        @pl.when((pl.program_id(0) == 0) & (pl.program_id(1) == 0))
        def _():
            copies = held.copies(starts_ref, refs, rest[n_held + 4 : n_held + 7])
            for some in copies:
                run_all(some, "start")
            for some in copies:
                run_all(some, "wait")

        @pl.when(pl.program_id(1) == 0)
        def _():
            sum_ref[...] = jnp.zeros_like(sum_ref)

        alive = live_ref[pl.program_id(0)].astype(jnp.float32)
        da = dot(du_ref[0], wu[...], 1, 1)
        unit_h, inv_h = normed(h_ref[0])
        unit_z, inv_z = normed(z_ref[0])
        dh1 = alive * c_ref[0] + norm_back(da, unit_h, inv_h, g_ref[2:3])
        dh_ref[0] = dh1
        dz = norm_back(dh1, unit_z, inv_z, g_ref[1:2]).astype(jnp.bfloat16)
        dz_ref[0] = dz
        do_ref[0] = dot(dz, wp[...], 1, 1).astype(jnp.bfloat16)
        sum_ref[0, 0:1] += jnp.sum(dh1 * unit_z, axis=0, keepdims=True)
        sum_ref[0, 1:2] += jnp.sum(da * unit_h, axis=0, keepdims=True)

    rows, per_slot, whole = token_specs(h1.shape, block)
    wide = pl.BlockSpec((1, block, hidden), lambda s, i, *_: (s, i, 0))
    low = jax.ShapeDtypeStruct(h1.shape, jnp.bfloat16)
    return pl.pallas_call(
        kernel,
        grid_spec=pltpu.PrefetchScalarGridSpec(
            num_scalar_prefetch=2,
            grid=(slots, length // block),
            in_specs=[wide, rows, rows, rows, whole(gains)] + held.in_specs,
            out_specs=[rows, rows, rows, per_slot(8)],
            scratch_shapes=held.scratch,
        ),
        out_shape=[
            low,
            low,
            jax.ShapeDtypeStruct(h1.shape, jnp.float32),
            jax.ShapeDtypeStruct((slots, 8, width), jnp.float32),
        ],
        compiler_params=params(),
        name="back_to_mixture",
    )(held.starts, live, du, h1, z, cotangent, gains, *held.refs)


def project_back(slot, part_of, groups, tokens, grad_middle, added, gain, weights, before=None):
    slots, length, width = tokens.shape
    block = row_block(length // part_of[1], 272)
    held = Weights(weights)
    per_weight = len(groups) // len(weights)
    n_held = len(held.refs)
    n_before = 0 if before is None else 2

    n_groups, part = len(groups), groups[0].shape[-1]
    steps = length // part_of[1] // block
    skip = part_of[0] * steps

    def kernel(starts_ref, *refs_in):
        d_refs, (x_ref, h_ref, e_ref, g_ref), rest = refs_in[:n_groups], refs_in[n_groups : n_groups + 4], refs_in[n_groups + 4 :]
        refs, rest = rest[:n_held], rest[n_held + n_before :]
        (out_ref, sum_ref), scratch = rest[:2], rest[2:]
        first = pl.program_id(0) == 0
        copies = sum(held.copies(starts_ref, refs, scratch), [])

        @pl.when(first)
        def _():
            run_all(copies, "start")

        unit, inv_std = normed(x_ref[0] + e_ref[0])

        @pl.when(first)
        def _():
            run_all(copies, "wait")

        da = None
        for w in range(len(weights)):
            mine = d_refs[w * per_weight : (w + 1) * per_weight]
            for i in range(3):
                more = dot(jnp.concatenate([ref[i, 0] for ref in mine], axis=1), scratch[w][i], 1, 1)
                da = more if da is None else da + more
        dh = h_ref[0] + norm_back(da, unit, inv_std, g_ref[...])
        out_ref[0] = dh

        @pl.when(pl.program_id(0) == 0)
        def _():
            sum_ref[...] = jnp.zeros_like(sum_ref)

        sum_ref[0, 0:1] += jnp.sum(da * unit, axis=0, keepdims=True)
        sum_ref[0, 1:2] += jnp.sum(dh, axis=0, keepdims=True)

    rows = pl.BlockSpec((1, block, width), lambda i, _: (slot, skip + i, 0))
    return pl.pallas_call(
        kernel,
        grid_spec=pltpu.PrefetchScalarGridSpec(
            num_scalar_prefetch=1,
            grid=(steps,),
            in_specs=[pl.BlockSpec((3, 1, block, part), lambda i, _: (0, slot, skip + i, 0))] * n_groups
            + [
                rows,
                rows,
                pl.BlockSpec((1, 1, width), lambda i, _: (slot, 0, 0)),
                pl.BlockSpec((1, width), lambda i, _: (0, 0)),
            ]
            + held.in_specs
            + [pl.BlockSpec(memory_space=pl.ANY)] * n_before,
            out_specs=[
                rows,
                pl.BlockSpec((1, 8, width), lambda i, _: (slot * 2 + part_of[0], 0, 0)),
            ],
            scratch_shapes=held.scratch,
        ),
        out_shape=[
            jax.ShapeDtypeStruct(tokens.shape, jnp.float32),
            jax.ShapeDtypeStruct((slots * 2, 8, width), jnp.float32),
        ],
        input_output_aliases={5 + n_groups + n_held + i: i for i in range(n_before)},
        compiler_params=params(),
        name="project_back",
    )(held.starts, *groups, tokens, grad_middle, added, gain, *held.refs, *(before or ()))


def columns_of(refs):
    if len(refs[0].shape) == 3:
        return jnp.concatenate([ref[0] for ref in refs], axis=1)
    return refs[0][...]


def grad_blocks(order, left, right, received=None):
    rows, depth = left.shape[0], left.shape[1] // 4
    tall = min(depth, 512)
    per_block = depth // tall
    stacked = isinstance(right, list)
    if stacked:
        count, slab = right[0].shape[0], sum(r.shape[-1] for r in right)
        right_specs = [pl.BlockSpec((1, rows, r.shape[-1]), lambda r, k, j, order: (j, 0, 0)) for r in right]
    else:
        slab = min(1024, right.shape[1])
        count = right.shape[1] // slab
        right_specs = [pl.BlockSpec((rows, slab), lambda r, k, j, order: (0, j))]
        right = [right]
    n_right = len(right)
    if depth <= 512:
        return narrow_grad_blocks(order, left, right, right_specs, (count, depth, slab), received)

    def kernel(order_ref, a_ref, *rest):
        right_block = columns_of(rest[:n_right])
        outs = rest[n_right:]
        total = dot(a_ref[...], right_block, 0, 0)
        if received is None:
            outs[0][0, 0] = total.astype(jnp.bfloat16)
            return
        total = (total + outs[0][0, 0].astype(jnp.float32)).astype(jnp.bfloat16)

        @pl.when(pl.program_id(0) == 0)
        def _():
            outs[1][0] = total

        @pl.when(pl.program_id(0) == 1)
        def _():
            outs[2][0] = total

    both = pl.BlockSpec((1, 1, tall, slab), lambda r, k, j, order: (r, j, k, 0))
    sent = pl.BlockSpec((1, tall, slab), lambda r, k, j, order: (jnp.where(r == 0, j, count - 1), jnp.where(r == 0, k, per_block - 1), 0))
    kept = pl.BlockSpec((1, tall, slab), lambda r, k, j, order: (jnp.where(r == 0, 0, j), jnp.where(r == 0, 0, k), 0))
    more = [] if received is None else [received]
    shape = (count, depth, slab)
    return pl.pallas_call(
        kernel,
        grid_spec=pltpu.PrefetchScalarGridSpec(
            num_scalar_prefetch=1,
            grid=(2, per_block, count),
            in_specs=[pl.BlockSpec((rows, tall), lambda r, k, j, order: (0, order[r] * per_block + k))]
            + right_specs
            + [both] * len(more),
            out_specs=[sent, kept] if more else both,
        ),
        out_shape=[jax.ShapeDtypeStruct(shape, jnp.bfloat16)] * 2 if more else jax.ShapeDtypeStruct((2,) + shape, jnp.bfloat16),
        compiler_params=params(),
        name="grad_blocks",
    )(order, left, *right, *more)


def narrow_grad_blocks(order, left, right, right_specs, shape, received):
    count, depth, slab = shape
    rows, n_right = left.shape[0], len(right)

    def kernel(order_ref, a0_ref, a1_ref, *rest):
        right_block = columns_of(rest[:n_right])
        outs = rest[n_right:]
        for r, a_ref in enumerate((a0_ref, a1_ref)):
            total = dot(a_ref[...], right_block, 0, 0)
            if received is None:
                outs[0][r, 0] = total.astype(jnp.bfloat16)
            else:
                outs[1 + r][0] = (total + outs[0][r, 0].astype(jnp.float32)).astype(jnp.bfloat16)

    by_step = lambda spec: pl.BlockSpec(spec.block_shape, lambda j, order: spec.index_map(0, 0, j, order))
    both = pl.BlockSpec((2, 1, depth, slab), lambda j, order: (0, j, 0, 0))
    one = pl.BlockSpec((1, depth, slab), lambda j, order: (j, 0, 0))
    left_spec = lambda r: pl.BlockSpec((rows, depth), lambda j, order: (0, order[r]), pipeline_mode=pl.Buffered(1))
    more = [] if received is None else [received]
    return pl.pallas_call(
        kernel,
        grid_spec=pltpu.PrefetchScalarGridSpec(
            num_scalar_prefetch=1,
            grid=(count,),
            in_specs=[left_spec(0), left_spec(1)] + [by_step(spec) for spec in right_specs] + [both] * len(more),
            out_specs=[one, one] if more else both,
        ),
        out_shape=[jax.ShapeDtypeStruct(shape, jnp.bfloat16)] * 2 if more else jax.ShapeDtypeStruct((2,) + shape, jnp.bfloat16),
        compiler_params=params(),
        name="grad_blocks",
    )(order, left, left, *right, *more)


def after(value, *earlier):
    return lax.optimization_barrier((value,) + earlier)[0]


def swap(value, axis, bit):
    size = lax.axis_size(axis)
    return lax.ppermute(value, axis, [(i, i ^ (1 << bit)) for i in range(size)])


def bit_of(axis, bit):
    return (lax.axis_index(axis) >> bit) & 1


def bits_of(axis):
    return range(lax.axis_size(axis).bit_length() - 1)


def pick(value, index):
    return lax.dynamic_index_in_dim(value, index, 0, keepdims=False)


def paired():
    return lax.axis_size("fsdp") == 2 and lax.axis_size("dp") % 2 == 0


def slot(before, ends=(), starts=()):
    before = tuple(before)
    if not paired():
        for e in ends:
            e.take()
        return before
    if ends:
        arrived = lax.optimization_barrier(tuple(e.received for e in ends) + before)
        for e, value in zip(ends, arrived):
            e.received = value
            e.take()
        before = arrived[len(ends) :]
    if starts:
        leaving = lax.optimization_barrier(tuple(e.sent for e in starts) + before)
        for e, value in zip(starts, leaving):
            e.send(value)
        before = leaving
    return before


class Gather:
    def __init__(self, low, ranges=None):
        self.low, self.ranges = low, ranges
        self.size, wide = low.shape
        whole = self.size * lax.axis_size("fsdp")
        self.shape = (whole, wide) if ranges is None else (len(ranges), whole, ranges[0][1] - ranges[0][0])
        self.crossed = None
        if paired():
            half = self.size // 2
            mine = lambda lo, hi: lax.dynamic_slice(low, (bit_of("dp", 0) * half, lo), (half, hi - lo))
            self.sent = mine(0, wide) if ranges is None else jnp.stack([mine(lo, hi) for lo, hi in ranges])
        else:
            self.sent = low

    def send(self, value):
        self.received = swap(value, "fsdp" if self.crossed is None else "dp", 0)

    def take(self):
        if not paired():
            return
        if self.crossed is None:
            self.crossed = self.sent = self.received
        else:
            self.beside = self.received

    def parts(self):
        ranges = () if self.ranges is None else (self.ranges,)
        if not paired():
            return [(lax.all_gather(self.low, "fsdp", axis=0, tiled=True), 0) + ranges], self.shape
        size, c, x = self.size, bit_of("dp", 0), lax.axis_index("fsdp")
        base = (1 - x) * size
        own = (self.low, x * size) + ranges
        return [own, (self.crossed, base + c * (size // 2)), (self.beside, base + (1 - c) * (size // 2))], self.shape


class WideGather:
    def __init__(self, low):
        self.low = low
        self.shape = (low.shape[0] * lax.axis_size("fsdp"), low.shape[1])
        self.crossed = None
        self.sent = low
        if paired():
            n_dp = lax.axis_size("dp")
            self.sent = pick(low.reshape(n_dp, low.shape[0] // n_dp, low.shape[1]), lax.axis_index("dp"))

    def send(self, value):
        if self.crossed is None:
            self.received = swap(value, "fsdp", 0)
        else:
            self.other = lax.all_gather(value, "dp", axis=0, tiled=True)

    def take(self):
        if paired():
            self.crossed = self.sent = self.received

    def parts(self):
        if not paired():
            return [(lax.all_gather(self.low, "fsdp", axis=0, tiled=True), 0)], self.shape
        size, x = self.low.shape[0], lax.axis_index("fsdp")
        return [(self.low, x * size), (self.other, (1 - x) * size)], self.shape


class Columns:
    def __init__(self, low):
        self.low = self.sent = low

    def send(self, value):
        self.received = swap(value, "fsdp", 0)

    def take(self):
        if not paired():
            self.whole = lax.all_gather(self.low, "fsdp", axis=1, tiled=True)
            return
        first = lax.axis_index("fsdp") == 0
        self.whole = jnp.concatenate(
            [jnp.where(first, self.low, self.received), jnp.where(first, self.received, self.low)], axis=1
        )


class SmallSum:
    def __init__(self, value):
        self.value, self.bits = value, None
        if paired():
            halves = value.reshape(value.shape[0], 2, -1)
            x = lax.axis_index("fsdp")
            self.value = lax.dynamic_index_in_dim(halves, x, 1, keepdims=False)
            self.sent = lax.dynamic_index_in_dim(halves, 1 - x, 1, keepdims=False)

    def send(self, value):
        if self.bits is None:
            self.bits = list(bits_of("dp"))
            self.received = swap(value, "fsdp", 0)
        else:
            self.received = swap(value, "dp", self.bits.pop(0))

    def take(self):
        if paired():
            self.value = self.sent = self.value + self.received

    def result(self):
        if paired():
            return self.value
        return lax.psum(lax.psum_scatter(self.value, "fsdp", scatter_dimension=1, tiled=True), "dp")


def assemble(pieces):
    count, rows, wide = pieces[0][0].shape
    n_pieces = len(pieces)

    def kernel(c_ref, *refs):
        out_ref = refs[-1]
        for p in range(n_pieces):

            @pl.when(pl.program_id(1) == p)
            def _():
                for i, ref in enumerate(refs[2 * p : 2 * p + 2]):
                    half = c_ref[0] if i == 0 else 1 - c_ref[0]
                    out_ref[pl.ds(pl.multiple_of(half * rows, rows), rows), :] = ref[0].astype(jnp.float32)

    return pl.pallas_call(
        kernel,
        grid_spec=pltpu.PrefetchScalarGridSpec(
            num_scalar_prefetch=1,
            grid=(count, n_pieces),
            in_specs=[pl.BlockSpec((1, rows, wide), lambda i, p, c: (i, 0, 0))] * (2 * n_pieces),
            out_specs=pl.BlockSpec((2 * rows, wide), lambda i, p, c: (0, i * n_pieces + p)),
        ),
        out_shape=jax.ShapeDtypeStruct((2 * rows, count * n_pieces * wide), jnp.float32),
        compiler_params=params(),
        name="assemble",
    )(bit_of("dp", 0).astype(jnp.int32).reshape(1), *[v for piece in pieces for v in piece])


def in_rows(whole):
    n, count, rows, wide = whole.shape
    n_bits = n.bit_length() - 1
    step = min(wide, 512)

    def place(i):
        return sum(((i >> (n_bits - 1 - b)) & 1) << b for b in range(n_bits))

    def kernel(in_ref, out_ref):
        for i in range(n):
            out_ref[place(i) * rows : (place(i) + 1) * rows, :] = in_ref[i, 0].astype(jnp.float32)

    return pl.pallas_call(
        kernel,
        grid=(count, wide // step),
        in_specs=[pl.BlockSpec((n, 1, rows, step), lambda s, j: (0, s, 0, j))],
        out_specs=pl.BlockSpec((n * rows, step), lambda s, j: (0, s * (wide // step) + j)),
        out_shape=jax.ShapeDtypeStruct((n * rows, count * wide), jnp.float32),
        compiler_params=params(),
        name="in_rows",
    )(whole)


class GradSum:
    def __init__(self, left, right, spread=False):
        self.left, self.right, self.spread = left, right, spread
        self.state = "send"
        if paired():
            self.bits = list(bits_of("dp"))[1:]

    def part(self, before):
        if not paired():
            if self.state == "send":
                right = self.right
                if isinstance(right, list):
                    right = jnp.concatenate([r[i] for i in range(3) for r in right], axis=1)
                low = dot(self.left, right, 0, 0).astype(jnp.bfloat16)
                piece = lax.psum_scatter(low, ("fsdp", "dp"), scatter_dimension=0, tiled=True)
                self.total = lax.all_gather(piece, "dp", axis=0, tiled=True).astype(jnp.float32)
                self.state = "keep"
            return before
        c, x = bit_of("dp", 0), lax.axis_index("fsdp")
        left = after(self.left, *before)
        if self.state == "send":
            order = jnp.stack([(1 - x) * 2 + 1 - c, x * 2 + 1 - c]).astype(jnp.int32)
            self.sent = grad_blocks(order, left, self.right)
        else:
            order = jnp.stack([(1 - x) * 2 + c, x * 2 + c]).astype(jnp.int32)
            self.sent, self.kept = grad_blocks(order, left, self.right, self.received)
        return (self.sent,)

    def send(self, value):
        if self.state == "send":
            self.received = swap(value, "dp", 0)
        elif self.state == "keep":
            self.received = swap(value, "fsdp", 0)
        elif self.state == "halve":
            self.received = swap(value, "dp", self.bit)
        elif self.spread:
            self.whole = lax.all_gather(value, "dp", axis=0, tiled=False)
        else:
            self.received = swap(value, "dp", self.bit)

    def take(self):
        if not paired():
            return
        if self.state == "send":
            self.state = "keep"
        elif self.state in ("keep", "halve"):
            if self.bits:
                self.state, self.bit = "halve", self.bits.pop(0)
                b = bit_of("dp", self.bit)
                slabs, rows, wide = self.kept.shape
                kept, received = (v.reshape(slabs, 2, rows // 2, wide) for v in (self.kept, self.received))
                part = lambda v, i: lax.dynamic_index_in_dim(v, i, 1, keepdims=False).astype(jnp.float32)
                self.sent = (part(kept, 1 - b) + part(received, 1 - b)).astype(jnp.bfloat16)
                self.kept = (part(kept, b) + part(received, b)).astype(jnp.bfloat16)
            else:
                self.kept = self.sent = (self.kept.astype(jnp.float32) + self.received.astype(jnp.float32)).astype(jnp.bfloat16)
                self.state, self.bits = "join", list(bits_of("dp"))
                self.bit = self.bits.pop()
        elif self.bits:
            self.kept = self.sent = in_order(self.kept, self.received, bit_of("dp", self.bit))
            self.bit = self.bits.pop()
        else:
            self.state = "done"

    def result(self, *earlier):
        if not paired():
            return self.total
        if self.spread:
            return in_rows(after(self.whole, *earlier))
        return assemble([(after(self.kept, *earlier), self.received)])


def in_order(mine, other, bit):
    return jnp.where(bit == 0, jnp.concatenate([mine, other], axis=1), jnp.concatenate([other, mine], axis=1))


def local(tokens, cotangent, group_ids, counts, w_qkv, w_proj, w_up, w_down, gains, table):
    slots, length, width = tokens.shape
    rows = slots * length
    flat = lambda v: v.reshape(v.shape[:-3] + (rows, v.shape[-1]))
    pairs = width // LANES
    n_groups = 2
    group_pairs = pairs // n_groups
    half = group_pairs // 2
    part = width // n_groups
    small = Columns(jnp.concatenate([gains, table], axis=0).astype(jnp.bfloat16))
    low_qkv = w_qkv.astype(jnp.bfloat16)
    get_qkv = [
        Gather(low_qkv, [(i * width + j * part, i * width + (j + 1) * part) for i in range(3)]) for j in range(n_groups)
    ]
    t = slot((), starts=[small, get_qkv[0]])
    get_down = WideGather(after(w_down, *t).astype(jnp.bfloat16))
    get_proj = Gather(after(w_proj, *t).astype(jnp.bfloat16))
    get_up = Gather(after(w_up, *t).astype(jnp.bfloat16))
    t = (get_down.sent, get_proj.sent, get_up.sent)
    t = slot(t, [small])
    small = small.whole.astype(jnp.float32)
    g = small[: gains.shape[0]]
    embed = small[gains.shape[0] :]
    onehot = (group_ids[:, None] == jnp.arange(table.shape[0])[None, :]).astype(jnp.float32)
    added = jnp.sum(onehot[:, :, None] * embed[None], axis=1)[:, None, :]
    live = (jnp.arange(slots) < counts[0]).astype(jnp.int32)
    a1 = norm_in(after(tokens, *t), added, g[0:1])
    t = slot((a1,), [get_qkv[0]], [get_qkv[0], get_qkv[1], get_down])
    t = slot(t, [get_qkv[0]])

    qkv = []
    group = project_in(after(a1, *t), get_qkv[0].parts())
    qkv.append(group)
    t = slot((group,), [get_qkv[1], get_down], [get_qkv[1], get_down, get_up, get_proj])
    attended = attn_fwd(after(group, *t), 0, group_pairs, 0, width)
    t = slot((attended[0],), [get_qkv[1]])
    group = project_in(after(a1, *t), get_qkv[1].parts())
    qkv.append(group)
    mixture, log_totals = attn_fwd(group, 0, group_pairs, group_pairs, width, attended)
    t = slot((mixture,), [get_up, get_proj], [get_up, get_proj])
    t = slot(t, [get_up, get_proj])
    p_qkv = [w.parts() for w in get_qkv]
    p_proj, p_up, p_down = get_proj.parts(), get_up.parts(), get_down.parts()
    a3, f, du, dm, z, h1, output, sums_out = up_and_down(
        live, after(mixture, *t), tokens, cotangent, added, g, p_proj, p_up, p_down
    )

    down = GradSum(flat(f), flat(dm), spread=True)
    up = GradSum(flat(a3), flat(du), spread=True)
    t = slot(down.part((dm,)), [], [down])
    t = slot(up.part(t), [down], [up])
    t = slot(down.part(t), [up], [down])
    t = up.part(t)
    dz, do, dh1, sums_mid = back_to_mixture(live, after(du, *t), h1, z, cotangent, g, p_proj, p_up)
    t = slot((dz,), [down], [down, up])
    proj = GradSum(flat(mixture), flat(dz))
    t = slot(proj.part(t), [], [proj])
    chunks = []

    def attend(i, t):
        group = i // 2
        chunks.append(attn_bwd(qkv[group], mixture, after(do, *t), log_totals, (i % 2) * half, half, group * group_pairs))
        return (chunks[-1],)

    t = attend(0, t)
    t = slot(t, [down, proj], [down])
    t = slot(proj.part(t), [], [proj])
    t = attend(1, t)
    t = slot(t, [up, down, proj], [up, down, proj])
    first = GradSum(flat(a1), [flat(d) for d in chunks])
    t = slot(first.part(t), [proj], [first, proj])
    t = attend(2, t)
    t = slot(t, [up, down, first, proj], [up, down, proj])
    t = slot(first.part(t), [proj], [first, proj])
    t = attend(3, t)
    t = slot(t, [up, first, proj], [up, first, proj])
    last = GradSum(flat(a1), [flat(d) for d in chunks[2:]])
    t = slot(last.part(t), [proj], [last, proj])
    grad_down = down.result(*t)
    t = slot((grad_down,), [last])
    t = slot(last.part(t), [up, first, proj], [up, last, first, proj])
    back = project_back(0, (0, 1), chunks, tokens, after(dh1, *t), added, g[0:1], p_qkv)
    t = slot((back[0],), [last, first, proj], [last, first])
    back = project_back(1, (0, 2), chunks, tokens, after(dh1, *t), added, g[0:1], p_qkv, back)
    t = slot((back[0],), [last, first], [last, first])
    back = project_back(1, (1, 2), chunks, tokens, after(dh1, *t), added, g[0:1], p_qkv, back)
    grad_tokens, more = back
    more = jnp.stack([more[0], more[2] + more[3]])
    grad_embed = jnp.sum(onehot[:, :, None] * more[:, None, 1, :], axis=0)
    grad_gains = jnp.concatenate([more[:, 0:1], sums_mid[:, 0:2], sums_out[:, 0:1]], axis=1).sum(axis=0)
    little = SmallSum(jnp.concatenate([grad_gains, grad_embed], axis=0))
    t = slot((more, little.sent) if paired() else (more,), [last, first], [last, first, little])
    grad_proj = proj.result(*t)
    t = slot((grad_proj,), [last, first, little], [last, first, little])
    grad_up = up.result(*t)
    t = (grad_up,)
    waiting = [last, first, little]
    while paired() and last.state != "done":
        t = slot(t, waiting)
        waiting = [e for e in (last, first) if e.state != "done"] + ([little] if little.bits else [])
        if waiting:
            t = slot(t, [], waiting)
    if paired():
        grad_qkv = assemble([(e.kept, e.received) for e in (first, last)])
    else:
        part = first.total.shape[1] // 3
        grad_qkv = jnp.concatenate([e.total[:, i * part : (i + 1) * part] for i in range(3) for e in (first, last)], axis=1)
    small_sum = little.result()
    return (
        output,
        grad_tokens,
        grad_qkv,
        grad_proj,
        grad_up,
        grad_down,
        small_sum[: gains.shape[0]],
        small_sum[gains.shape[0] :],
    )


def solution(mesh):
    by_seq = P(("dp", "fsdp"), None, None)
    by_slot = P(("dp", "fsdp"))
    by_row = P("fsdp", None)
    by_col = P(None, "fsdp")
    return jax.shard_map(
        local,
        mesh=mesh,
        in_specs=(by_seq, by_seq, by_slot, by_slot) + (by_row,) * 4 + (by_col,) * 2,
        out_specs=(by_seq, by_seq) + (by_row,) * 4 + (by_col,) * 2,
        check_vma=False,
    )
```
